512 devices in a mesh: section: 2 (over x_lo), chan: 128 (over y, z, core), win: 2 (over x_hi).
Axes of the slice: x: 4 (x_hi: 2, x_lo: 2; x = x_hi * 2 + x_lo), y: 4, z: 16, core: 2. Of those that a mesh axis runs over, the one named last changes fastest.
Arguments:
- raw: bfloat16 [8, 1024, 640], P(('section', 'win'), 'chan'), may hold values from -6 to 6
- flags: int32 [8, 1024], P(('section', 'win'), 'chan'), may hold values from 0 to 1, as said below
- in_weight: bfloat16 [32, 3], replicated, may hold values from -3.5 to 3.5
- conv_weight: bfloat16 [3, 32, 32, 3, 3], replicated, may hold values from -0.375 to 0.375
- out_weight: bfloat16 [32], replicated, may hold values from -1 to 1
- sources: int32 [128], replicated, may hold values from 0 to 1023
Outputs:
- coherency: float32 [256, 2, 128, 1024], P(('section', 'chan'), None, None, 'win')
The draws below stay inside these ranges and needn't reach their ends.
Inputs may be any that keep to these rules, and one draw needn't show every extreme that they name: `flags`: some channels have no valid window at all, and some exactly one.
All inputs are finite; a program needn't handle non-finite values.
Results may differ from the reference program's by a relative error of at most 0.04.
Values may be sent and summed in bfloat16 or wider, within the bound.
No kernel may reach another device: no remote copies, remote signals or barrier semaphores. Data moves between devices by JAX's collectives and lax.ppermute only.
A program may use at most 64 MiB of HBM per device.

```python
import math
import jax
import jax.numpy as jnp
from jax import lax

NT = 640
F = 32
LAYERS = 3
NF = 256
NV = 128
CH = 1024
WINS = 8


def draw_flags(key, part):
    base_key = jax.random.fold_in(key, 71)
    order_key = jax.random.fold_in(key, 72)
    lone_key = jax.random.fold_in(key, 73)
    base = jax.random.randint(base_key, (WINS, CH), 0, 2).astype(jnp.int32)
    order = jax.random.permutation(order_key, CH).astype(jnp.int32)
    roles = jnp.zeros((CH,), jnp.int32)
    roles = roles.at[order[0:3]].set(1)
    roles = roles.at[order[3:11]].set(2)
    lone = jax.random.randint(lone_key, (CH,), 0, WINS).astype(jnp.int32)
    single = (jnp.arange(WINS, dtype=jnp.int32)[:, None] == lone[None, :]).astype(jnp.int32)
    chosen = jnp.where(roles[None, :] == 2, single, base)
    return jnp.where(roles[None, :] == 1, jnp.zeros_like(chosen), chosen).astype(jnp.int32)


def place_ends(values, stream_key, smallest, largest):
    place = [jax.random.randint(jax.random.fold_in(stream_key, axis), (), 0, length) for axis, length in enumerate(values.shape)]
    longest = values.shape.index(max(values.shape))
    beside = place[:longest] + [(place[longest] + 1) % values.shape[longest]] + place[longest + 1:]
    return values.at[tuple(place)].set(smallest).at[tuple(beside)].set(largest)


def block_scale(own_key, shape, pieces, smallest, top_value):
    gain, own = 1.0, jax.random.fold_in(own_key, 6)
    for position, shards_of in pieces:
        steps = jnp.exp(jax.random.uniform(jax.random.fold_in(own, position), (shards_of,), jnp.float32, smallest / len(pieces), top_value / len(pieces)))
        gain = gain * jnp.repeat(steps, shape[position] // shards_of).reshape([-1 if axis == position else 1 for axis in range(len(shape))])
    return gain


def centred(rng, extent, deviation, most, shards=(), kind=jnp.bfloat16):
    drawn = deviation * jax.random.normal(rng, extent, jnp.float32)
    if shards:
        drawn = drawn * block_scale(rng, extent, shards, -0.22, 0.18)
    return jnp.clip(drawn, -most, most).astype(kind)


def setup_inputs(seed: int = 0) -> dict:
    streams_of = jax.random.split(jax.random.key(seed), 7)
    raw = centred(streams_of[0], (WINS, CH, NT), 1.0, 6.0, ((0, 4), (1, 128)))
    flags = draw_flags(jax.random.fold_in(streams_of[6], 71), 0)
    in_weight = centred(streams_of[2], (F, 3), 3 ** -0.5, 3.5)
    conv_weight = centred(streams_of[3], (LAYERS, F, F, 3, 3), (9 * F) ** -0.5, 0.375)
    out_weight = centred(streams_of[4], (F,), F ** -0.5, 1.0)
    sources = place_ends(jax.random.randint(streams_of[5], (NV,), 0, CH), jax.random.fold_in(streams_of[5], 1), 0, CH - 1).astype(jnp.int32)
    return {"raw": raw, "flags": flags, "in_weight": in_weight, "conv_weight": conv_weight, "out_weight": out_weight, "sources": sources}


water_level = 0.2
epsilon_power = 1e-06

def dft_table(samples, bin_count):
    sample_index = jnp.arange(samples, dtype=jnp.int32)[:, None]
    bin_index = jnp.arange(1, bin_count + 1, dtype=jnp.int32)[None, :]
    phases = sample_index * bin_index % samples
    angles = phases.astype(jnp.float32) * (2.0 * math.pi / samples)
    return jnp.concatenate([jnp.cos(angles), -jnp.sin(angles)], axis=1).astype(jnp.bfloat16)

def input_layer(traces, in_weight):
    length = traces.shape[-1]
    padded = jnp.pad(traces.astype(jnp.float32), ((0, 0), (0, 0), (1, 1)))
    weights = in_weight.astype(jnp.float32)
    result = padded[:, None, :, 0:length] * weights[None, :, 0, None, None]
    result = result + padded[:, None, :, 1:length + 1] * weights[None, :, 1, None, None]
    result = result + padded[:, None, :, 2:length + 2] * weights[None, :, 2, None, None]
    return result.astype(jnp.bfloat16)

def dilated_conv(padded, weight, dilation):
    return lax.conv_general_dilated(padded, weight, (1, 1), ((0, 0), (dilation, dilation)), rhs_dilation=(1, dilation), dimension_numbers=('NCHW', 'OIHW', 'NCHW'), preferred_element_type=jnp.float32)

def whiten(spectra, flag_rows):
    bin_count = spectra.shape[1] // 2
    real_part = spectra[:, :bin_count]
    imag_part = spectra[:, bin_count:]
    band_power = real_part * real_part + imag_part * imag_part
    spread = jnp.sqrt(lax.optimization_barrier(jnp.mean(band_power, axis=1, keepdims=True)) + epsilon_power)
    factor = flag_rows.astype(jnp.float32)[:, None] / (jnp.sqrt(band_power) + water_level * spread)
    return jnp.stack([real_part * factor, imag_part * factor], axis=1).astype(jnp.bfloat16)

def coherence(source_rows, receiver_rows):
    src_re = source_rows[:, :, 0, :].astype(jnp.float32)
    src_im = source_rows[:, :, 1, :].astype(jnp.float32)
    rec_re = receiver_rows[:, :, 0, :].astype(jnp.float32)
    rec_im = receiver_rows[:, :, 1, :].astype(jnp.float32)
    cross_re = jnp.einsum('wvf,wcf->fvc', src_re, rec_re) + jnp.einsum('wvf,wcf->fvc', src_im, rec_im)
    cross_im = jnp.einsum('wvf,wcf->fvc', src_re, rec_im) - jnp.einsum('wvf,wcf->fvc', src_im, rec_re)
    energy_src = jnp.einsum('wvf,wvf->fv', src_re, src_re) + jnp.einsum('wvf,wvf->fv', src_im, src_im)
    energy_rec = jnp.einsum('wcf,wcf->fc', rec_re, rec_re) + jnp.einsum('wcf,wcf->fc', rec_im, rec_im)
    denominator = jnp.sqrt(jnp.maximum(energy_src[:, :, None] * energy_rec[:, None, :], 1.0))
    return jnp.stack([cross_re, cross_im], axis=1) / denominator[:, None, :, :]

def reference(raw, flags, in_weight, conv_weight, out_weight, sources):
    table = dft_table(NT, NF)

    def one_window(inputs):
        traces, flag_rows = inputs
        hidden = input_layer(traces[None], in_weight)
        for layer_index in range(LAYERS):
            padded = jnp.pad(hidden, ((0, 0), (0, 0), (1, 1), (0, 0)))
            conv_out = dilated_conv(padded, conv_weight[layer_index], 2 ** layer_index)
            hidden = (hidden.astype(jnp.float32) + jax.nn.relu(conv_out)).astype(jnp.bfloat16)
        clean = jnp.einsum('wfct,f->wct', hidden.astype(jnp.float32), out_weight.astype(jnp.float32)).astype(jnp.bfloat16)
        spectra = jnp.dot(clean.reshape(-1, NT), table, preferred_element_type=jnp.float32)
        return whiten(spectra, flag_rows)
    whitened = lax.map(one_window, (raw, flags))
    chosen = jnp.take(whitened, sources.astype(jnp.int32), axis=1)
    return coherence(chosen, whitened)
```

```python
import functools
import math

import jax
import jax.numpy as jnp
import numpy as np
from jax import lax
from jax.experimental import pallas as pl
from jax.experimental.pallas import tpu as pltpu
from jax.sharding import Mesh, PartitionSpec as P

NT = 640
F = 32
LAYERS = 3
NF = 256
OWN = 8
WIN = 2
EXT = OWN + 2 * LAYERS
BLK = 6
WIDE = WIN * NT

water_level = 0.2
epsilon_power = 1e-06

F32 = jnp.float32
BF16 = jnp.bfloat16


def dft_table():
    part, z, core, y, section = np.meshgrid(
        np.arange(2), np.arange(16), np.arange(2), np.arange(4), np.arange(2), indexing="ij"
    )
    k = (section * 128 + (y * 16 + z) * 2 + core).reshape(-1)
    part = part.reshape(-1)
    phases = np.arange(NT)[:, None] * (k + 1)[None, :] % NT
    angles = phases.astype(np.float32) * np.float32(2.0 * math.pi / NT)
    table = np.where(part[None, :] == 0, np.cos(angles), -np.sin(angles))
    return table.astype(BF16)


def iota(shape, dim):
    return lax.broadcasted_iota(jnp.int32, shape, dim)


def column(row, n):
    eye = iota((n, n), 0) == iota((n, n), 1)
    return jnp.sum(jnp.where(eye, jnp.broadcast_to(row, (n, n)), 0.0), axis=1, keepdims=True)


def swap_bits(x, row_step, lane_step):
    rows, lanes = x.shape
    row_bit = (iota(x.shape, 0) // row_step) % 2
    lane_bit = (iota(x.shape, 1) // lane_step) % 2
    down = pltpu.roll(pltpu.roll(x, rows - row_step, 0), lane_step, 1)
    up = pltpu.roll(pltpu.roll(x, row_step, 0), lanes - lane_step, 1)
    return jnp.where(row_bit == lane_bit, x, jnp.where(row_bit == 0, down, up))


def prepare_kernel(conv_ref, in_ref, out_ref, band_ref, first_ref, last_ref):
    for layer in range(LAYERS):
        for tap in range(3):
            taps = [conv_ref[layer, a, tap].astype(F32) for a in range(3)]
            base = jnp.concatenate(taps + [jnp.zeros((F, 256 - 3 * F), F32)], axis=1)
            for c in range(BLK):
                row = base if c == 0 else pltpu.roll(base, F * c, 1)
                band_ref[layer, tap, F * c : F * (c + 1), :] = row.astype(BF16)
    shape = (EXT * F, 72)
    channel = iota(shape, 0) // F
    place = jnp.where(channel < 3, 13 + channel, jnp.where(channel < 11, channel - 3, channel + 5))
    lane = iota(shape, 1)
    first = jnp.zeros(shape, F32)
    for tap in range(3):
        weight = column(in_ref[tap : tap + 1, :].astype(F32), F)
        tall = jnp.broadcast_to(jnp.concatenate([weight] * EXT, axis=0), shape)
        first = jnp.where(lane == place + 24 * tap, tall, first)
    first_ref[...] = first.astype(BF16)
    shape = (OWN, OWN * F)
    wide = jnp.concatenate([out_ref[...].astype(F32)] * OWN, axis=1)
    last_ref[...] = jnp.where(
        iota(shape, 0) == iota(shape, 1) // F, jnp.broadcast_to(wide, shape), 0.0
    ).astype(BF16)


def shifted(x, step):
    time = iota(x.shape, 1) % NT
    moved = pltpu.roll(x, step % WIDE, 1)
    keep = (time >= step) if step > 0 else (time < NT + step)
    return jnp.where(keep, moved, jnp.zeros_like(moved))


def denoise_kernel(
    edge_ref, left_ref, raw_ref, right_ref, flags_ref, band_ref, first_ref, last_ref, table_ref,
    out_ref, taps_ref, next_ref, line_ref,
):
    is_first, is_last = edge_ref[0], edge_ref[1]
    rows = jnp.concatenate(
        [
            jnp.concatenate([ref[w].astype(F32) for w in range(WIN)], axis=1)
            for ref in (raw_ref, left_ref, right_ref)
        ],
        axis=0,
    )
    lines = jnp.concatenate([shifted(rows, 1), rows, shifted(rows, -1)], axis=0).astype(BF16)
    for n in range(0, WIDE, 256):
        next_ref[:, n : n + 256] = jnp.dot(
            first_ref[...], lines[:, n : n + 256], preferred_element_type=F32
        ).astype(BF16)
    count = EXT
    for layer in range(LAYERS):
        step = 2**layer
        for r in range(0, count * F, F):
            block = next_ref[r : r + F, :].astype(F32)
            taps_ref[0, r : r + F, :] = shifted(block, step).astype(BF16)
            taps_ref[1, r : r + F, :] = next_ref[r : r + F, :]
            taps_ref[2, r : r + F, :] = shifted(block, -step).astype(BF16)
        count -= 2
        for c in range(0, count, BLK):
            size = min(BLK, count - c)
            for n in range(0, WIDE, 256):
                total = None
                for tap in range(3):
                    term = jnp.dot(
                        band_ref[layer, tap, : size * F, : (size + 2) * F],
                        taps_ref[tap, c * F : (c + size + 2) * F, n : n + 256],
                        preferred_element_type=F32,
                    )
                    total = term if total is None else total + term
                old = taps_ref[1, (c + 1) * F : (c + 1 + size) * F, n : n + 256].astype(F32)
                new = old + jnp.maximum(total, 0.0)
                reach = LAYERS - 1 - layer
                for k in range(size):
                    part = new[k * F : (k + 1) * F]
                    if c + k < reach:
                        part = jnp.where(is_first == 1, 0.0, part)
                    if c + k >= count - reach:
                        part = jnp.where(is_last == 1, 0.0, part)
                    next_ref[(c + k) * F : (c + k + 1) * F, n : n + 256] = part.astype(BF16)
    clean = jnp.dot(last_ref[...], next_ref[: OWN * F, :], preferred_element_type=F32)
    clean = jnp.concatenate([clean[:, w * NT : (w + 1) * NT] for w in range(WIN)], axis=0)
    spectra = jnp.dot(clean.astype(BF16), table_ref[...], preferred_element_type=F32)
    real, imag = spectra[:, :NF], spectra[:, NF:]
    power = real * real + imag * imag
    spread = jnp.sqrt(jnp.mean(power, axis=1, keepdims=True) + epsilon_power)
    flags = jnp.concatenate(
        [column(flags_ref[w : w + 1, :].astype(F32), OWN) for w in range(WIN)], axis=0
    )
    factor = flags / (jnp.sqrt(power) + water_level * spread)
    for part, value in enumerate((real * factor, imag * factor)):
        for w in range(WIN):
            for high in range(2):
                x = value[w * OWN : (w + 1) * OWN, high * 128 : (high + 1) * 128]
                for bit in range(3):
                    x = swap_bits(x, 2**bit, 16 * 2**bit)
                line_ref[pl.ds(32 * high + 2 * w + part, 8, stride=4), :] = x
    out_ref[...] = line_ref[...].astype(BF16)


def turn_kernel(in_ref, out_ref):
    x = in_ref[...].astype(F32)
    for bit in range(4):
        x = swap_bits(x, 4 * 2**bit, 2**bit)
    x = x.astype(BF16)
    out_ref[:64, :] = x
    out_ref[64:, :] = x


def coherence_kernel(half_ref, sources_ref, in_ref, out_ref, all_ref):
    x = in_ref[...].astype(F32)

    def piece(w, c, y):
        start = ((w * 2 + c) * 4 + y) * 8
        return x[start : start + 8]

    stacked = jnp.concatenate(
        [
            jnp.concatenate([piece(w, c, y) for y in range(4) for w in range(2)], axis=0)
            for c in range(2)
        ],
        axis=1,
    ).astype(BF16)
    shape = (256, 256)
    r = iota(shape, 0)
    target = (r % 16) * 16 + (r // 128) * 8 + (r // 16) % 8
    perm = jnp.where(target == iota(shape, 1), 1.0, 0.0).astype(BF16)
    ordered = jnp.dot(stacked, perm, preferred_element_type=F32)
    every = jnp.concatenate([ordered[16 * y : 16 * (y + 1)] for y in range(4)], axis=1)
    all_ref[...] = every
    half = half_ref[0]
    receivers = all_ref[:, pl.ds(pl.multiple_of(half * 512, 512), 512)]
    shape = (CH_ALL, 128)
    one_hot = jnp.where(
        iota(shape, 0) == jnp.broadcast_to(sources_ref[...], shape), 1.0, 0.0
    ).astype(BF16)
    chosen = jnp.dot(every.astype(BF16), one_hot, preferred_element_type=F32)
    even = iota(receivers.shape, 0) % 2 == 0
    turned = jnp.where(even, pltpu.roll(receivers, 15, 0), -pltpu.roll(receivers, 1, 0))
    chosen_t = chosen.T
    energy_src = jnp.sum(chosen_t * chosen_t, axis=1, keepdims=True)
    energy_rec = jnp.sum(receivers * receivers, axis=0, keepdims=True)
    scale = lax.rsqrt(jnp.maximum(energy_src * energy_rec, 1.0))
    left = chosen_t.astype(BF16)
    out_ref[0, 0] = jnp.dot(left, receivers.astype(BF16), preferred_element_type=F32) * scale
    out_ref[0, 1] = jnp.dot(left, turned.astype(BF16), preferred_element_type=F32) * scale


CH_ALL = 1024

VMEM = pl.BlockSpec(memory_space=pltpu.VMEM)
SMEM = pl.BlockSpec(memory_space=pltpu.SMEM)
PARAMS = pltpu.CompilerParams(vmem_limit_bytes=32 * 1024 * 1024)


def prepare(conv_weight, in_weight, out_weight):
    return pl.pallas_call(
        prepare_kernel,
        out_shape=(
            jax.ShapeDtypeStruct((LAYERS, 3, BLK * F, 256), BF16),
            jax.ShapeDtypeStruct((EXT * F, 72), BF16),
            jax.ShapeDtypeStruct((OWN, OWN * F), BF16),
        ),
        in_specs=[VMEM] * 3,
        out_specs=(VMEM,) * 3,
        compiler_params=PARAMS,
        cost_estimate=pl.CostEstimate(flops=2_000_000, bytes_accessed=2_000_000, transcendentals=0),
        name="prepare",
    )(conv_weight.transpose(0, 3, 4, 1, 2), in_weight.T, out_weight.reshape(1, F))


def denoise(edge, left, raw, right, flags, band, first, last, table):
    return pl.pallas_call(
        denoise_kernel,
        out_shape=jax.ShapeDtypeStruct((64, 128), BF16),
        in_specs=[SMEM] + [VMEM] * 8,
        out_specs=VMEM,
        scratch_shapes=[
            pltpu.VMEM((3, EXT * F, WIDE), BF16),
            pltpu.VMEM((EXT * F, WIDE), BF16),
            pltpu.VMEM((64, 128), F32),
        ],
        compiler_params=PARAMS,
        name="denoise",
    )(edge, left, raw, right, flags, band, first, last, table)


def turn(rows):
    return pl.pallas_call(
        turn_kernel,
        out_shape=jax.ShapeDtypeStruct((128, 128), BF16),
        in_specs=[VMEM],
        out_specs=VMEM,
        compiler_params=PARAMS,
        name="turn",
    )(rows)


def coherence(half, sources, rows):
    return pl.pallas_call(
        coherence_kernel,
        out_shape=jax.ShapeDtypeStruct((1, 2, 128, 512), F32),
        in_specs=[SMEM, VMEM, VMEM],
        out_specs=VMEM,
        scratch_shapes=[pltpu.VMEM((16, CH_ALL), F32)],
        compiler_params=PARAMS,
        name="coherence",
    )(half, sources.reshape(1, 128), rows)


CHAN = ("y", "z", "c")


def per_device(raw, flags, in_weight, conv_weight, out_weight, sources):
    count = lax.axis_size(CHAN)
    me = lax.axis_index(CHAN)
    left = lax.ppermute(raw, CHAN, [(i, i + 1) for i in range(count - 1)])
    right = lax.ppermute(raw, CHAN, [(i + 1, i) for i in range(count - 1)])
    edge = jnp.stack([me == 0, me == count - 1]).astype(jnp.int32)
    half = lax.axis_index("w").reshape(1).astype(jnp.int32)
    band, first, last = prepare(conv_weight, in_weight, out_weight)
    table = jnp.asarray(dft_table())
    sent = denoise(edge, left, raw, right, flags, band, first, last, table)
    got = lax.all_to_all(sent, "z", 0, 0, tiled=True)
    turned = turn(got)
    mine = lax.all_to_all(turned, ("w", "c", "y", "s"), 0, 0, tiled=True)
    return coherence(half, sources, mine)


def solution(mesh):
    fine = Mesh(mesh.devices.reshape(2, 4, 16, 2, 2), ("s", "y", "z", "c", "w"))
    placed = (P(("s", "w"), CHAN, None), P(("s", "w"), CHAN), P(), P(), P(), P())
    return jax.shard_map(
        per_device,
        mesh=fine,
        in_specs=placed,
        out_specs=P(("s",) + CHAN, None, None, "w"),
        check_vma=False,
    )
```

```python
import functools
import math

import jax
import jax.numpy as jnp
import numpy as np
from jax import lax
from jax.experimental import pallas as pl
from jax.experimental.pallas import tpu as pltpu
from jax.sharding import Mesh, PartitionSpec as P

NT = 640
F = 32
LAYERS = 3
NF = 256
OWN = 8
WIN = 2
EXT = OWN + 2 * LAYERS
BLK = 6
WIDE = WIN * NT

water_level = 0.2
epsilon_power = 1e-06

F32 = jnp.float32
BF16 = jnp.bfloat16


def dft_table():
    part, z, core, y, section = np.meshgrid(
        np.arange(2), np.arange(16), np.arange(2), np.arange(4), np.arange(2), indexing="ij"
    )
    k = (section * 128 + (y * 16 + z) * 2 + core).reshape(-1)
    part = part.reshape(-1)
    phases = np.arange(NT)[:, None] * (k + 1)[None, :] % NT
    angles = phases.astype(np.float32) * np.float32(2.0 * math.pi / NT)
    table = np.where(part[None, :] == 0, np.cos(angles), -np.sin(angles))
    return table.astype(BF16)


def iota(shape, dim):
    return lax.broadcasted_iota(jnp.int32, shape, dim)


def column(row, n):
    eye = iota((n, n), 0) == iota((n, n), 1)
    return jnp.sum(jnp.where(eye, jnp.broadcast_to(row, (n, n)), 0.0), axis=1, keepdims=True)


def swap_bits(x, row_step, lane_step):
    rows, lanes = x.shape
    row_bit = (iota(x.shape, 0) // row_step) % 2
    lane_bit = (iota(x.shape, 1) // lane_step) % 2
    down = pltpu.roll(pltpu.roll(x, rows - row_step, 0), lane_step, 1)
    up = pltpu.roll(pltpu.roll(x, row_step, 0), lanes - lane_step, 1)
    return jnp.where(row_bit == lane_bit, x, jnp.where(row_bit == 0, down, up))


def prepare_kernel(
    conv_any, in_any, out_any, table_any, raw_any, flags_any, sources_any,
    band_ref, first_ref, last_ref, table_ref, raw_ref, flags_ref, sources_ref,
    conv_ref, in_ref, out_ref, sems,
):
    pairs = (
        (conv_any, conv_ref), (in_any, in_ref), (out_any, out_ref), (raw_any, raw_ref),
        (flags_any, flags_ref), (sources_any, sources_ref), (table_any, table_ref),
    )
    copies = [pltpu.make_async_copy(a, b, sems.at[i]) for i, (a, b) in enumerate(pairs)]
    for copy in copies:
        copy.start()
    copies[1].wait()
    shape = (EXT * F, 72)
    channel = iota(shape, 0) // F
    place = jnp.where(channel < 3, 13 + channel, jnp.where(channel < 11, channel - 3, channel + 5))
    lane = iota(shape, 1)
    first = jnp.zeros(shape, F32)
    for tap in range(3):
        weight = column(in_ref[tap : tap + 1, :].astype(F32), F)
        tall = jnp.broadcast_to(jnp.concatenate([weight] * EXT, axis=0), shape)
        first = jnp.where(lane == place + 24 * tap, tall, first)
    first_ref[...] = first.astype(BF16)
    copies[2].wait()
    shape = (OWN, OWN * F)
    wide = jnp.concatenate([out_ref[...].astype(F32)] * OWN, axis=1)
    last_ref[...] = jnp.where(
        iota(shape, 0) == iota(shape, 1) // F, jnp.broadcast_to(wide, shape), 0.0
    ).astype(BF16)
    copies[0].wait()
    for layer in range(LAYERS):
        for tap in range(3):
            taps = [conv_ref[layer, a, tap] for a in range(3)]
            base = jnp.concatenate(taps + [jnp.zeros((F, 256 - 3 * F), BF16)], axis=1)
            for c in range(BLK):
                row = base if c == 0 else pltpu.roll(base, F * c, 1)
                band_ref[layer, F * c : F * (c + 1), 256 * tap : 256 * (tap + 1)] = row
    for copy in copies[3:]:
        copy.wait()


def shifted(x, step):
    time = iota(x.shape, 1) % NT
    moved = pltpu.roll(x, step % WIDE, 1)
    keep = (time >= step) if step > 0 else (time < NT + step)
    return jnp.where(keep, moved, jnp.zeros_like(moved))


def denoise_kernel(
    edge_ref, near_ref, raw_ref, far_ref, flags_ref, band_ref, first_ref, last_ref, table_ref,
    out_ref, h0_ref, h1_ref, h2_ref, h3_ref, taps_ref, line_ref,
):
    is_first, is_last, odd = edge_ref[0], edge_ref[1], edge_ref[2]
    own, near, far = (
        jnp.concatenate([ref[w].astype(F32) for w in range(WIN)], axis=1)
        for ref in (raw_ref, near_ref, far_ref)
    )
    rows = jnp.concatenate(
        [own, jnp.where(odd == 1, near, far), jnp.where(odd == 1, far, near)], axis=0
    )
    lines = jnp.concatenate([shifted(rows, 1), rows, shifted(rows, -1)], axis=0).astype(BF16)
    hidden = (h0_ref, h1_ref, h2_ref, h3_ref)

    def input_chunk(n):
        h0_ref[:, n * 256 : (n + 1) * 256] = jnp.dot(
            first_ref[...], lines[:, n * 256 : (n + 1) * 256], preferred_element_type=F32
        ).astype(BF16)

    def taps_column(layer, j):
        step = 2**layer
        source = hidden[layer]
        size = (EXT - 2 * layer) * F
        lane = iota((size, 128), 1)
        here = source[:, j * 128 : (j + 1) * 128]
        zero = jnp.zeros_like(here)
        inside = j % 5
        before = zero if inside == 0 else pltpu.roll(source[:, (j - 1) * 128 : j * 128], step, 1)
        taps_ref[0, :size, j * 128 : (j + 1) * 128] = jnp.where(
            lane < step, before, pltpu.roll(here, step, 1)
        )
        after = zero if inside == 4 else pltpu.roll(source[:, (j + 1) * 128 : (j + 2) * 128], 128 - step, 1)
        taps_ref[1, :size, j * 128 : (j + 1) * 128] = jnp.where(
            lane >= 128 - step, after, pltpu.roll(here, 128 - step, 1)
        )

    def layer_chunk(layer, n):
        source, target = hidden[layer], hidden[layer + 1]
        count = EXT - 2 * (layer + 1)
        reach = LAYERS - 1 - layer
        cols = slice(n * 256, (n + 1) * 256)
        taps_column(layer, 2 * n)
        taps_column(layer, 2 * n + 1)
        for start, low in ((0, 0), (count - BLK, 2 * BLK - count)):
            k = slice(start * F, (start + BLK + 2) * F)
            window = jnp.concatenate([taps_ref[0, k, cols], source[k, cols], taps_ref[1, k, cols]], axis=0)
            total = jnp.dot(band_ref[layer, low * F :, :], window, preferred_element_type=F32)
            old = source[(start + low + 1) * F : (start + BLK + 1) * F, cols].astype(F32)
            new = old + jnp.maximum(total, 0.0)
            for i in range(BLK - low):
                c = start + low + i
                part = new[i * F : (i + 1) * F]
                if c < reach:
                    part = jnp.where(is_first == 1, 0.0, part)
                if c >= count - reach:
                    part = jnp.where(is_last == 1, 0.0, part)
                target[c * F : (c + 1) * F, cols] = part.astype(BF16)

    chunks = WIDE // 256
    for n in range(chunks + LAYERS):
        if n < chunks:
            input_chunk(n)
        for layer in range(LAYERS):
            if 0 <= n - layer - 1 < chunks:
                layer_chunk(layer, n - layer - 1)
    clean = jnp.dot(last_ref[...], h3_ref[...], preferred_element_type=F32)
    clean = jnp.concatenate([clean[:, w * NT : (w + 1) * NT] for w in range(WIN)], axis=0)
    spectra = jnp.dot(clean.astype(BF16), table_ref[...], preferred_element_type=F32)
    real, imag = spectra[:, :NF], spectra[:, NF:]
    power = real * real + imag * imag
    spread = jnp.sqrt(jnp.mean(power, axis=1, keepdims=True) + epsilon_power)
    flags = jnp.concatenate(
        [column(flags_ref[w : w + 1, :].astype(F32), OWN) for w in range(WIN)], axis=0
    )
    factor = flags / (jnp.sqrt(power) + water_level * spread)
    for part, value in enumerate((real * factor, imag * factor)):
        for w in range(WIN):
            for high in range(2):
                x = value[w * OWN : (w + 1) * OWN, high * 128 : (high + 1) * 128]
                for bit in range(3):
                    x = swap_bits(x, 2**bit, 16 * 2**bit)
                line_ref[pl.ds(32 * high + 2 * w + part, 8, stride=4), :] = x
    out_ref[...] = line_ref[...].astype(BF16)


def turn_kernel(in_ref, out_ref):
    x = in_ref[...].astype(F32)
    for bit in range(4):
        x = swap_bits(x, 4 * 2**bit, 2**bit)
    x = x.astype(BF16)
    out_ref[:64, :] = x
    out_ref[64:, :] = x


def coherence_kernel(half_ref, sources_ref, in_ref, out_any, all_ref, out_ref, sems):
    x = in_ref[...].astype(F32)

    def piece(w, c, y):
        start = ((w * 2 + c) * 4 + y) * 8
        return x[start : start + 8]

    stacked = jnp.concatenate(
        [
            jnp.concatenate([piece(w, c, y) for y in range(4) for w in range(2)], axis=0)
            for c in range(2)
        ],
        axis=1,
    ).astype(BF16)
    shape = (256, 256)
    r = iota(shape, 0)
    target = (r % 16) * 16 + (r // 128) * 8 + (r // 16) % 8
    perm = jnp.where(target == iota(shape, 1), 1.0, 0.0).astype(BF16)
    ordered = jnp.dot(stacked, perm, preferred_element_type=F32)
    every = jnp.concatenate([ordered[16 * y : 16 * (y + 1)] for y in range(4)], axis=1)
    all_ref[...] = every
    half = half_ref[0]
    receivers = all_ref[:, pl.ds(pl.multiple_of(half * 512, 512), 512)]
    shape = (CH_ALL, 128)
    one_hot = jnp.where(
        iota(shape, 0) == jnp.broadcast_to(sources_ref[...], shape), 1.0, 0.0
    ).astype(BF16)
    chosen = jnp.dot(every.astype(BF16), one_hot, preferred_element_type=F32)
    even = iota(receivers.shape, 0) % 2 == 0
    turned = jnp.where(even, pltpu.roll(receivers, 15, 0), -pltpu.roll(receivers, 1, 0))
    chosen_t = chosen.T
    energy_src = jnp.sum(chosen_t * chosen_t, axis=1, keepdims=True)
    energy_rec = jnp.sum(receivers * receivers, axis=0, keepdims=True)
    scale = lax.rsqrt(jnp.maximum(energy_src * energy_rec, 1.0))
    left = chosen_t.astype(BF16)
    copies = []
    for part, right in enumerate((receivers, turned)):
        out_ref[part] = jnp.dot(left, right.astype(BF16), preferred_element_type=F32) * scale
        copies.append(pltpu.make_async_copy(out_ref.at[part], out_any.at[0, part], sems.at[part]))
        copies[-1].start()
    for copy in copies:
        copy.wait()


CH_ALL = 1024

VMEM = pl.BlockSpec(memory_space=pltpu.VMEM)
SMEM = pl.BlockSpec(memory_space=pltpu.SMEM)
PARAMS = pltpu.CompilerParams(vmem_limit_bytes=32 * 1024 * 1024)


def prepare(conv_weight, in_weight, out_weight, table, raw, flags, sources):
    arrays = (
        conv_weight.transpose(0, 3, 4, 1, 2), in_weight.T, out_weight.reshape(1, F),
        table, raw, flags, sources.reshape(1, -1),
    )
    arrays = tuple(pltpu.with_memory_space_constraint(a, pltpu.HBM) for a in arrays)
    return pl.pallas_call(
        prepare_kernel,
        out_shape=(
            jax.ShapeDtypeStruct((LAYERS, BLK * F, 3 * 256), BF16),
            jax.ShapeDtypeStruct((EXT * F, 72), BF16),
            jax.ShapeDtypeStruct((OWN, OWN * F), BF16),
        )
        + tuple(jax.ShapeDtypeStruct(a.shape, a.dtype) for a in arrays[3:]),
        in_specs=[pl.BlockSpec(memory_space=pl.ANY)] * 7,
        out_specs=(VMEM,) * 7,
        scratch_shapes=[pltpu.VMEM(a.shape, a.dtype) for a in arrays[:3]]
        + [pltpu.SemaphoreType.DMA((7,))],
        compiler_params=PARAMS,
        cost_estimate=pl.CostEstimate(flops=2_000_000, bytes_accessed=4_000_000, transcendentals=0),
        name="prepare",
    )(*arrays)


def denoise(edge, near, raw, far, flags, band, first, last, table):
    return pl.pallas_call(
        denoise_kernel,
        out_shape=jax.ShapeDtypeStruct((64, 128), BF16),
        in_specs=[SMEM] + [VMEM] * 8,
        out_specs=VMEM,
        scratch_shapes=[pltpu.VMEM(((EXT - 2 * i) * F, WIDE), BF16) for i in range(LAYERS + 1)]
        + [pltpu.VMEM((2, EXT * F, WIDE), BF16), pltpu.VMEM((64, 128), F32)],
        compiler_params=PARAMS,
        name="denoise",
    )(edge, near, raw, far, flags, band, first, last, table)


def turn(rows):
    return pl.pallas_call(
        turn_kernel,
        out_shape=jax.ShapeDtypeStruct((128, 128), BF16),
        in_specs=[VMEM],
        out_specs=VMEM,
        compiler_params=PARAMS,
        name="turn",
    )(rows)


def coherence(half, sources, rows):
    return pl.pallas_call(
        coherence_kernel,
        out_shape=jax.ShapeDtypeStruct((1, 2, 128, 512), F32),
        in_specs=[SMEM, VMEM, VMEM],
        out_specs=pl.BlockSpec(memory_space=pl.ANY),
        scratch_shapes=[
            pltpu.VMEM((16, CH_ALL), F32),
            pltpu.VMEM((2, 128, 512), F32),
            pltpu.SemaphoreType.DMA((2,)),
        ],
        compiler_params=PARAMS,
        name="coherence",
    )(half, sources, rows)


CHAN = ("y", "z", "c")


def per_device(raw, flags, in_weight, conv_weight, out_weight, sources):
    count = lax.axis_size(CHAN)
    me = lax.axis_index(CHAN)
    odd = lax.axis_index("c")
    across = [(i, i + 1) for i in range(1, count - 1, 2)]
    far = lax.ppermute(raw, CHAN, across + [(b, a) for a, b in across])
    near = lax.ppermute(raw, "c", [(0, 1), (1, 0)])
    edge = jnp.stack([me == 0, me == count - 1, odd == 1]).astype(jnp.int32)
    half = lax.axis_index("w").reshape(1).astype(jnp.int32)
    band, first, last, table, raw, flags, sources = prepare(
        conv_weight, in_weight, out_weight, jnp.asarray(dft_table()), raw, flags, sources
    )
    sent = denoise(edge, near, raw, far, flags, band, first, last, table)
    half, sources, sent = lax.optimization_barrier((half, sources, sent))
    got = lax.all_to_all(sent, "z", 0, 0, tiled=True)
    mine = lax.all_to_all(turn(got), ("w", "c", "y", "s"), 0, 0, tiled=True)
    return coherence(half, sources, mine)


def solution(mesh):
    fine = Mesh(mesh.devices.reshape(2, 4, 16, 2, 2), ("s", "y", "z", "c", "w"))
    placed = (P(("s", "w"), CHAN, None), P(("s", "w"), CHAN), P(), P(), P(), P())
    return jax.shard_map(
        per_device,
        mesh=fine,
        in_specs=placed,
        out_specs=P(("s",) + CHAN, None, None, "w"),
        check_vma=False,
    )
```

```python
import functools
import math

import jax
import jax.numpy as jnp
import numpy as np
from jax import lax
from jax.experimental import pallas as pl
from jax.experimental.pallas import tpu as pltpu
from jax.sharding import Mesh, PartitionSpec as P

NT = 640
F = 32
LAYERS = 3
NF = 256
OWN = 8
WIN = 2
EXT = OWN + 2 * LAYERS
BLK = 6
LANES = 128
PH = NT // LANES
CHUNK = WIN * LANES
WIDE = WIN * NT
CH_ALL = 1024
NV = 128

water_level = 0.2
epsilon_power = 1e-06

F32 = jnp.float32
BF16 = jnp.bfloat16


def dft_table():
    part, z, core, y, section = np.meshgrid(
        np.arange(2), np.arange(16), np.arange(2), np.arange(4), np.arange(2), indexing="ij"
    )
    k = (section * 128 + (y * 16 + z) * 2 + core).reshape(-1)
    part = part.reshape(-1)
    phases = np.arange(NT)[:, None] * (k + 1)[None, :] % NT
    angles = phases.astype(np.float32) * np.float32(2.0 * math.pi / NT)
    table = np.where(part[None, :] == 0, np.cos(angles), -np.sin(angles))
    return table[sample_order()].astype(BF16)


def sample_order():
    return (np.arange(LANES)[None, :] * PH + np.arange(PH)[:, None]).reshape(-1)


def sample_perm():
    return np.eye(NT, dtype=np.float32)[:, sample_order()].astype(BF16)


def channel_perm():
    core, channel, z = np.meshgrid(np.arange(2), np.arange(OWN), np.arange(16), indexing="ij")
    target = ((z * 2 + core) * OWN + channel).reshape(-1)
    return np.eye(256, dtype=np.float32)[target].astype(BF16)


def iota(shape, dim):
    return lax.broadcasted_iota(jnp.int32, shape, dim)


def column(row, n):
    eye = iota((n, n), 0) == iota((n, n), 1)
    return jnp.sum(jnp.where(eye, jnp.broadcast_to(row, (n, n)), 0.0), axis=1, keepdims=True)


def swap_bits(x, row_step, lane_step):
    rows, lanes = x.shape
    row_bit = (iota(x.shape, 0) // row_step) % 2
    lane_bit = (iota(x.shape, 1) // lane_step) % 2
    down = pltpu.roll(pltpu.roll(x, rows - row_step, 0), lane_step, 1)
    up = pltpu.roll(pltpu.roll(x, row_step, 0), lanes - lane_step, 1)
    return jnp.where(row_bit == lane_bit, x, jnp.where(row_bit == 0, down, up))


def prepare_kernel(
    conv_any, in_any, out_any, sources_any, raw_any, flags_any, order_any, table_any, perm_any,
    band_ref, first_ref, last_ref, one_hot_ref, raw_ref, flags_ref, order_ref, table_ref, perm_ref,
    conv_ref, in_ref, out_ref, sources_ref, sems,
):
    pairs = (
        (conv_any, conv_ref), (in_any, in_ref), (out_any, out_ref), (sources_any, sources_ref),
        (raw_any, raw_ref), (flags_any, flags_ref), (order_any, order_ref), (table_any, table_ref),
        (perm_any, perm_ref),
    )
    copies = [pltpu.make_async_copy(a, b, sems.at[i]) for i, (a, b) in enumerate(pairs)]
    for copy in copies:
        copy.start()
    copies[1].wait()
    shape = (EXT * F, 72)
    channel = iota(shape, 0) // F
    place = jnp.where(channel < 3, 13 + channel, jnp.where(channel < 11, channel - 3, channel + 5))
    lane = iota(shape, 1)
    first = jnp.zeros(shape, F32)
    for tap in range(3):
        weight = column(in_ref[tap : tap + 1, :].astype(F32), F)
        tall = jnp.broadcast_to(jnp.concatenate([weight] * EXT, axis=0), shape)
        first = jnp.where(lane == place + 24 * tap, tall, first)
    first_ref[...] = first.astype(BF16)
    copies[2].wait()
    shape = (OWN, OWN * F)
    wide = jnp.concatenate([out_ref[...].astype(F32)] * OWN, axis=1)
    last_ref[...] = jnp.where(
        iota(shape, 0) == iota(shape, 1) // F, jnp.broadcast_to(wide, shape), 0.0
    ).astype(BF16)
    copies[3].wait()
    shape = (CH_ALL, NV)
    one_hot_ref[...] = jnp.where(
        iota(shape, 0) == jnp.broadcast_to(sources_ref[...], shape), 1.0, 0.0
    ).astype(BF16)
    copies[0].wait()
    for layer in range(LAYERS):
        for tap in range(3):
            taps = [conv_ref[layer, a, tap] for a in range(3)]
            base = jnp.concatenate(taps + [jnp.zeros((F, 256 - 3 * F), BF16)], axis=1)
            for c in range(BLK):
                row = base if c == 0 else pltpu.roll(base, F * c, 1)
                band_ref[layer, F * c : F * (c + 1), 256 * tap : 256 * (tap + 1)] = row
    for copy in copies[4:]:
        copy.wait()


def lane_shift(x, step):
    edge = iota((x.shape[0], LANES), 1) == (0 if step == 1 else LANES - 1)
    moved = [
        jnp.where(edge, jnp.zeros_like(part), pltpu.roll(part, step % LANES, 1))
        for part in (x[:, i : i + LANES] for i in range(0, x.shape[1], LANES))
    ]
    return jnp.concatenate(moved, axis=1)


def denoise_kernel(
    edge_ref, near_ref, raw_ref, far_ref, flags_ref, order_ref, band_ref, first_ref, last_ref, table_ref,
    out_ref, h0_ref, h1_ref, h2_ref, h3_ref, earlier_ref, later_ref, line_ref,
):
    is_first, is_last, odd = edge_ref[0], edge_ref[1], edge_ref[2]
    near, far = near_ref[...].astype(F32), far_ref[...].astype(F32)
    left, right = jnp.where(odd == 1, near, far), jnp.where(odd == 1, far, near)
    rows = [x for w in range(WIN) for x in (raw_ref[w].astype(F32), left[w], right[w])]
    rows = jnp.concatenate(rows, axis=0).astype(BF16)
    rows = jnp.dot(rows, order_ref[...], preferred_element_type=F32)
    lines = [
        jnp.concatenate(
            [rows[24 * w : 24 * (w + 1), v * LANES : (v + 1) * LANES] for w in range(WIN)], axis=1
        )
        for v in range(PH)
    ]
    hidden = (h0_ref, h1_ref, h2_ref, h3_ref)
    chunk = [slice(v * CHUNK, (v + 1) * CHUNK) for v in range(PH)]
    for v in range(PH):
        before = lines[v - 1] if v > 0 else lane_shift(lines[PH - 1], 1)
        after = lines[v + 1] if v < PH - 1 else lane_shift(lines[0], -1)
        taps = jnp.concatenate([before, lines[v], after], axis=0).astype(BF16)
        h0_ref[:, chunk[v]] = jnp.dot(first_ref[...], taps, preferred_element_type=F32).astype(BF16)
    for layer in range(LAYERS):
        step = 2**layer
        source, target = hidden[layer], hidden[layer + 1]
        size = (EXT - 2 * layer) * F
        count = EXT - 2 * (layer + 1)
        reach = LAYERS - 1 - layer
        for v in sorted(range(PH), key=lambda v: (v < step) + (v >= PH - step)):
            before, after, u, t = source, source, v - step, v + step
            if u < 0:
                u += PH
                before = earlier_ref
                earlier_ref[:size, chunk[u]] = lane_shift(source[:, chunk[u]], 1)
            if t >= PH:
                t -= PH
                after = later_ref
                later_ref[:size, chunk[t]] = lane_shift(source[:, chunk[t]], -1)
            for start, low in ((0, 0), (count - BLK, 2 * BLK - count)):
                k = slice(start * F, (start + BLK + 2) * F)
                taps = jnp.concatenate([before[k, chunk[u]], source[k, chunk[v]], after[k, chunk[t]]], axis=0)
                total = jnp.dot(band_ref[layer, low * F :, :], taps, preferred_element_type=F32)
                old = source[(start + low + 1) * F : (start + BLK + 1) * F, chunk[v]].astype(F32)
                new = old + jnp.maximum(total, 0.0)
                for i in range(BLK - low):
                    c = start + low + i
                    part = new[i * F : (i + 1) * F]
                    if c < reach:
                        part = jnp.where(is_first == 1, 0.0, part)
                    if c >= count - reach:
                        part = jnp.where(is_last == 1, 0.0, part)
                    target[c * F : (c + 1) * F, chunk[v]] = part.astype(BF16)
    clean = jnp.dot(last_ref[...], h3_ref[...], preferred_element_type=F32)
    clean = jnp.concatenate(
        [
            jnp.concatenate(
                [clean[:, v * CHUNK + w * LANES : v * CHUNK + (w + 1) * LANES] for v in range(PH)], axis=1
            )
            for w in range(WIN)
        ],
        axis=0,
    )
    spectra = jnp.dot(clean.astype(BF16), table_ref[...], preferred_element_type=F32)
    real, imag = spectra[:, :NF], spectra[:, NF:]
    power = real * real + imag * imag
    spread = jnp.sqrt(jnp.mean(power, axis=1, keepdims=True) + epsilon_power)
    flags = jnp.concatenate(
        [column(flags_ref[w : w + 1, :].astype(F32), OWN) for w in range(WIN)], axis=0
    )
    factor = flags / (jnp.sqrt(power) + water_level * spread)
    for part, value in enumerate((real * factor, imag * factor)):
        for w in range(WIN):
            for high in range(2):
                x = value[w * OWN : (w + 1) * OWN, high * 128 : (high + 1) * 128]
                for bit in range(3):
                    x = swap_bits(x, 2**bit, 16 * 2**bit)
                line_ref[pl.ds(32 * high + 2 * w + part, 8, stride=4), :] = x
    out_ref[...] = line_ref[...].astype(BF16)


def turn_kernel(in_ref, out_ref):
    x = in_ref[...].astype(F32)
    for bit in range(4):
        x = swap_bits(x, 4 * 2**bit, 2**bit)
    x = x.astype(BF16)
    out_ref[:64, :] = x
    out_ref[64:, :] = x


def coherence_kernel(half_ref, one_hot_ref, perm_ref, in_ref, out_any, all_ref, out_ref, sems):
    x = in_ref[...].astype(F32)

    def piece(w, c, y):
        start = ((w * 2 + c) * 4 + y) * 8
        return x[start : start + 8]

    stacked = jnp.concatenate(
        [
            jnp.concatenate([piece(w, c, y) for y in range(4) for w in range(2)], axis=0)
            for c in range(2)
        ],
        axis=1,
    ).astype(BF16)
    ordered = jnp.dot(stacked, perm_ref[...], preferred_element_type=F32)
    every = jnp.concatenate([ordered[16 * y : 16 * (y + 1)] for y in range(4)], axis=1)
    all_ref[...] = every
    half = half_ref[0]
    receivers = all_ref[:, pl.ds(pl.multiple_of(half * 512, 512), 512)]
    chosen = jnp.dot(every.astype(BF16), one_hot_ref[...], preferred_element_type=F32)
    even = iota(receivers.shape, 0) % 2 == 0
    turned = jnp.where(even, pltpu.roll(receivers, 15, 0), -pltpu.roll(receivers, 1, 0))
    chosen_t = chosen.T
    energy_src = jnp.sum(chosen_t * chosen_t, axis=1, keepdims=True)
    energy_rec = jnp.sum(receivers * receivers, axis=0, keepdims=True)
    scale = lax.rsqrt(jnp.maximum(energy_src * energy_rec, 1.0))
    left = chosen_t.astype(BF16)
    copies = []
    for part, right in enumerate((receivers, turned)):
        out_ref[part] = jnp.dot(left, right.astype(BF16), preferred_element_type=F32) * scale
        copies.append(pltpu.make_async_copy(out_ref.at[part], out_any.at[0, part], sems.at[part]))
        copies[-1].start()
    for copy in copies:
        copy.wait()


VMEM = pl.BlockSpec(memory_space=pltpu.VMEM)
SMEM = pl.BlockSpec(memory_space=pltpu.SMEM)
PARAMS = pltpu.CompilerParams(vmem_limit_bytes=32 * 1024 * 1024)


def prepare(conv_weight, in_weight, out_weight, sources, raw, flags):
    arrays = (
        conv_weight.transpose(0, 3, 4, 1, 2), in_weight.T, out_weight.reshape(1, F), sources.reshape(1, NV),
        raw, flags, jnp.asarray(sample_perm()), jnp.asarray(dft_table()), jnp.asarray(channel_perm()),
    )
    arrays = tuple(pltpu.with_memory_space_constraint(a, pltpu.HBM) for a in arrays)
    return pl.pallas_call(
        prepare_kernel,
        out_shape=(
            jax.ShapeDtypeStruct((LAYERS, BLK * F, 3 * 256), BF16),
            jax.ShapeDtypeStruct((EXT * F, 72), BF16),
            jax.ShapeDtypeStruct((OWN, OWN * F), BF16),
            jax.ShapeDtypeStruct((CH_ALL, NV), BF16),
        )
        + tuple(jax.ShapeDtypeStruct(a.shape, a.dtype) for a in arrays[4:]),
        in_specs=[pl.BlockSpec(memory_space=pl.ANY)] * 9,
        out_specs=(VMEM,) * 9,
        scratch_shapes=[pltpu.VMEM(a.shape, a.dtype) for a in arrays[:4]]
        + [pltpu.SemaphoreType.DMA((9,))],
        compiler_params=PARAMS,
        cost_estimate=pl.CostEstimate(flops=2_000_000, bytes_accessed=4_000_000, transcendentals=0),
        name="prepare",
    )(*arrays)


def denoise(edge, near, raw, far, flags, order, band, first, last, table):
    return pl.pallas_call(
        denoise_kernel,
        out_shape=jax.ShapeDtypeStruct((64, 128), BF16),
        in_specs=[SMEM] + [VMEM] * 9,
        out_specs=VMEM,
        scratch_shapes=[pltpu.VMEM(((EXT - 2 * i) * F, WIDE), BF16) for i in range(LAYERS + 1)]
        + [pltpu.VMEM((EXT * F, WIDE), BF16)] * 2
        + [pltpu.VMEM((64, 128), F32)],
        compiler_params=PARAMS,
        name="denoise",
    )(edge, near, raw, far, flags, order, band, first, last, table)


def turn(rows):
    return pl.pallas_call(
        turn_kernel,
        out_shape=jax.ShapeDtypeStruct((128, 128), BF16),
        in_specs=[VMEM],
        out_specs=VMEM,
        compiler_params=PARAMS,
        name="turn",
    )(rows)


def coherence(half, one_hot, perm, rows):
    return pl.pallas_call(
        coherence_kernel,
        out_shape=jax.ShapeDtypeStruct((1, 2, 128, 512), F32),
        in_specs=[SMEM, VMEM, VMEM, VMEM],
        out_specs=pl.BlockSpec(memory_space=pl.ANY),
        scratch_shapes=[
            pltpu.VMEM((16, CH_ALL), F32),
            pltpu.VMEM((2, 128, 512), F32),
            pltpu.SemaphoreType.DMA((2,)),
        ],
        compiler_params=PARAMS,
        name="coherence",
    )(half, one_hot, perm, rows)


CHAN = ("y", "z", "c")


def per_device(raw, flags, in_weight, conv_weight, out_weight, sources):
    count = lax.axis_size(CHAN)
    me = lax.axis_index(CHAN)
    odd = lax.axis_index("c")
    across = [(i, i + 1) for i in range(1, count - 1, 2)]
    far = lax.ppermute(raw, CHAN, across + [(b, a) for a, b in across])
    near = lax.ppermute(raw, "c", [(0, 1), (1, 0)])
    edge = jnp.stack([me == 0, me == count - 1, odd == 1]).astype(jnp.int32)
    half = lax.axis_index("w").reshape(1).astype(jnp.int32)
    band, first, last, one_hot, raw, flags, order, table, perm = prepare(
        conv_weight, in_weight, out_weight, sources, raw, flags
    )
    sent = denoise(edge, near, raw, far, flags, order, band, first, last, table)
    half, sent = lax.optimization_barrier((half, sent))
    got = lax.all_to_all(sent, "z", 0, 0, tiled=True)
    mine = lax.all_to_all(turn(got), ("w", "c", "y", "s"), 0, 0, tiled=True)
    return coherence(half, one_hot, perm, mine)


def solution(mesh):
    fine = Mesh(mesh.devices.reshape(2, 4, 16, 2, 2), ("s", "y", "z", "c", "w"))
    placed = (P(("s", "w"), CHAN, None), P(("s", "w"), CHAN), P(), P(), P(), P())
    return jax.shard_map(
        per_device,
        mesh=fine,
        in_specs=placed,
        out_specs=P(("s",) + CHAN, None, None, "w"),
        check_vma=False,
    )
```

```python
import functools
import math

import jax
import jax.numpy as jnp
import numpy as np
from jax import lax
from jax.experimental import pallas as pl
from jax.experimental.pallas import tpu as pltpu
from jax.sharding import Mesh, PartitionSpec as P

NT = 640
F = 32
LAYERS = 3
NF = 256
OWN = 8
WIN = 2
EXT = OWN + 2 * LAYERS
BLK = 6
LANES = 128
PH = NT // LANES
CHUNK = WIN * LANES
WIDE = WIN * NT
CH_ALL = 1024
NV = 128
Y_ORDER = (2, 3, 0, 1)
W_ORDER = (1, 0)
Z_ORDER = tuple((np.arange(16) + 8) % 16)

water_level = 0.2
epsilon_power = 1e-06

F32 = jnp.float32
BF16 = jnp.bfloat16


def dft_table():
    part, z, core, y, section = np.meshgrid(
        np.arange(2), np.array(Z_ORDER), np.arange(2), np.array(Y_ORDER), np.arange(2), indexing="ij"
    )
    k = (section * 128 + (y * 16 + z) * 2 + core).reshape(-1)
    part = part.reshape(-1)
    phases = np.arange(NT)[:, None] * (k + 1)[None, :] % NT
    angles = phases.astype(np.float32) * np.float32(2.0 * math.pi / NT)
    table = np.where(part[None, :] == 0, np.cos(angles), -np.sin(angles))
    return table[sample_order()].astype(BF16)


def sample_order():
    return (np.arange(LANES)[None, :] * PH + np.arange(PH)[:, None]).reshape(-1)


def sample_perm():
    return np.eye(NT, dtype=np.float32)[:, sample_order()].astype(BF16)


def channel_perm():
    core, channel, z = np.meshgrid(np.arange(2), np.arange(OWN), np.array(Z_ORDER), indexing="ij")
    target = ((z * 2 + core) * OWN + channel).reshape(-1)
    return np.eye(256, dtype=np.float32)[target].astype(BF16)


def iota(shape, dim):
    return lax.broadcasted_iota(jnp.int32, shape, dim)


def column(row, n):
    eye = iota((n, n), 0) == iota((n, n), 1)
    return jnp.sum(jnp.where(eye, jnp.broadcast_to(row, (n, n)), 0.0), axis=1, keepdims=True)


def swap_bits(x, row_step, lane_step):
    rows, lanes = x.shape
    row_bit = (iota(x.shape, 0) // row_step) % 2
    lane_bit = (iota(x.shape, 1) // lane_step) % 2
    down = pltpu.roll(pltpu.roll(x, rows - row_step, 0), lane_step, 1)
    up = pltpu.roll(pltpu.roll(x, row_step, 0), lanes - lane_step, 1)
    return jnp.where(row_bit == lane_bit, x, jnp.where(row_bit == 0, down, up))


def prepare_kernel(
    conv_any, in_any, out_any, sources_any, raw_any, flags_any, order_any, table_any, perm_any,
    band_ref, first_ref, last_ref, one_hot_ref, raw_ref, flags_ref, order_ref, table_ref, perm_ref,
    conv_ref, in_ref, out_ref, sources_ref, sems,
):
    pairs = (
        (conv_any, conv_ref), (in_any, in_ref), (out_any, out_ref), (sources_any, sources_ref),
        (raw_any, raw_ref), (flags_any, flags_ref), (order_any, order_ref), (table_any, table_ref),
        (perm_any, perm_ref),
    )
    copies = [pltpu.make_async_copy(a, b, sems.at[i]) for i, (a, b) in enumerate(pairs)]
    for copy in copies:
        copy.start()
    copies[1].wait()
    shape = (EXT * F, 72)
    channel = iota(shape, 0) // F
    place = jnp.where(channel < 3, 13 + channel, jnp.where(channel < 11, channel - 3, channel + 5))
    lane = iota(shape, 1)
    first = jnp.zeros(shape, F32)
    for tap in range(3):
        weight = column(in_ref[tap : tap + 1, :].astype(F32), F)
        tall = jnp.broadcast_to(jnp.concatenate([weight] * EXT, axis=0), shape)
        first = jnp.where(lane == place + 24 * tap, tall, first)
    first_ref[...] = first.astype(BF16)
    copies[2].wait()
    shape = (OWN, OWN * F)
    wide = jnp.concatenate([out_ref[...].astype(F32)] * OWN, axis=1)
    last_ref[...] = jnp.where(
        iota(shape, 0) == iota(shape, 1) // F, jnp.broadcast_to(wide, shape), 0.0
    ).astype(BF16)
    copies[3].wait()
    shape = (CH_ALL, NV)
    one_hot_ref[...] = jnp.where(
        iota(shape, 0) == jnp.broadcast_to(sources_ref[...], shape), 1.0, 0.0
    ).astype(BF16)
    copies[0].wait()
    for layer in range(LAYERS):
        for tap in range(3):
            taps = [conv_ref[layer, a, tap] for a in range(3)]
            base = jnp.concatenate(taps + [jnp.zeros((F, 256 - 3 * F), BF16)], axis=1)
            for c in range(BLK):
                row = base if c == 0 else pltpu.roll(base, F * c, 1)
                band_ref[layer, F * c : F * (c + 1), 256 * tap : 256 * (tap + 1)] = row
    for copy in copies[4:]:
        copy.wait()


def lane_shift(x, step):
    edge = iota((x.shape[0], LANES), 1) == (0 if step == 1 else LANES - 1)
    moved = [
        jnp.where(edge, jnp.zeros_like(part), pltpu.roll(part, step % LANES, 1))
        for part in (x[:, i : i + LANES] for i in range(0, x.shape[1], LANES))
    ]
    return jnp.concatenate(moved, axis=1)


def denoise_kernel(
    edge_ref, far_ref, raw_ref, near_ref, flags_ref, order_ref, band_ref, first_ref, last_ref, table_ref,
    out_ref, h0_ref, h1_ref, h2_ref, h3_ref, earlier_ref, later_ref, line_ref,
):
    is_first, is_last, odd = edge_ref[0], edge_ref[1], edge_ref[2]
    near, far = near_ref[...].astype(F32), far_ref[...].astype(F32)
    left, right = jnp.where(odd == 1, near, far), jnp.where(odd == 1, far, near)
    rows = [x for w in range(WIN) for x in (raw_ref[w].astype(F32), left[w], right[w])]
    rows = jnp.concatenate(rows, axis=0).astype(BF16)
    rows = jnp.dot(rows, order_ref[...], preferred_element_type=F32)
    lines = [
        jnp.concatenate(
            [rows[24 * w : 24 * (w + 1), v * LANES : (v + 1) * LANES] for w in range(WIN)], axis=1
        )
        for v in range(PH)
    ]
    hidden = (h0_ref, h1_ref, h2_ref, h3_ref)
    chunk = [slice(v * CHUNK, (v + 1) * CHUNK) for v in range(PH)]
    for v in range(PH):
        before = lines[v - 1] if v > 0 else lane_shift(lines[PH - 1], 1)
        after = lines[v + 1] if v < PH - 1 else lane_shift(lines[0], -1)
        taps = jnp.concatenate([before, lines[v], after], axis=0).astype(BF16)
        h0_ref[:, chunk[v]] = jnp.dot(first_ref[...], taps, preferred_element_type=F32).astype(BF16)
    for layer in range(LAYERS):
        step = 2**layer
        source, target = hidden[layer], hidden[layer + 1]
        size = (EXT - 2 * layer) * F
        count = EXT - 2 * (layer + 1)
        reach = LAYERS - 1 - layer
        for v in sorted(range(PH), key=lambda v: (v < step) + (v >= PH - step)):
            before, after, u, t = source, source, v - step, v + step
            if u < 0:
                u += PH
                before = earlier_ref
                earlier_ref[:size, chunk[u]] = lane_shift(source[:, chunk[u]], 1)
            if t >= PH:
                t -= PH
                after = later_ref
                later_ref[:size, chunk[t]] = lane_shift(source[:, chunk[t]], -1)
            for start, low in ((0, 0), (count - BLK, 2 * BLK - count)):
                k = slice(start * F, (start + BLK + 2) * F)
                taps = jnp.concatenate([before[k, chunk[u]], source[k, chunk[v]], after[k, chunk[t]]], axis=0)
                total = jnp.dot(band_ref[layer, low * F :, :], taps, preferred_element_type=F32)
                old = source[(start + low + 1) * F : (start + BLK + 1) * F, chunk[v]].astype(F32)
                new = old + jnp.maximum(total, 0.0)
                for i in range(BLK - low):
                    c = start + low + i
                    part = new[i * F : (i + 1) * F]
                    if c < reach:
                        part = jnp.where(is_first == 1, 0.0, part)
                    if c >= count - reach:
                        part = jnp.where(is_last == 1, 0.0, part)
                    target[c * F : (c + 1) * F, chunk[v]] = part.astype(BF16)
    clean = jnp.dot(last_ref[...], h3_ref[...], preferred_element_type=F32)
    clean = jnp.concatenate(
        [
            jnp.concatenate(
                [clean[:, v * CHUNK + w * LANES : v * CHUNK + (w + 1) * LANES] for v in range(PH)], axis=1
            )
            for w in range(WIN)
        ],
        axis=0,
    )
    spectra = jnp.dot(clean.astype(BF16), table_ref[...], preferred_element_type=F32)
    real, imag = spectra[:, :NF], spectra[:, NF:]
    power = real * real + imag * imag
    spread = jnp.sqrt(jnp.mean(power, axis=1, keepdims=True) + epsilon_power)
    flags = jnp.concatenate(
        [column(flags_ref[w : w + 1, :].astype(F32), OWN) for w in range(WIN)], axis=0
    )
    factor = flags / (jnp.sqrt(power) + water_level * spread)
    for part, value in enumerate((real * factor, imag * factor)):
        for w in range(WIN):
            for high in range(2):
                x = value[w * OWN : (w + 1) * OWN, high * 128 : (high + 1) * 128]
                for bit in range(3):
                    x = swap_bits(x, 2**bit, 16 * 2**bit)
                line_ref[pl.ds(32 * high + 2 * w + part, 8, stride=4), :] = x
    out_ref[...] = line_ref[...].astype(BF16)


def turn_kernel(in_ref, out_ref):
    x = in_ref[...].astype(F32)
    for bit in range(4):
        x = swap_bits(x, 4 * 2**bit, 2**bit)
    x = x.astype(BF16)
    out_ref[:64, :] = x
    out_ref[64:, :] = x


def coherence_kernel(half_ref, one_hot_ref, perm_ref, in_ref, out_any, all_ref, out_ref, sems):
    x = in_ref[...].astype(F32)

    def piece(w, c, y):
        start = ((w * 2 + c) * 4 + Y_ORDER.index(y)) * 8
        return x[start : start + 8]

    stacked = jnp.concatenate(
        [
            jnp.concatenate([piece(w, c, y) for y in range(4) for w in range(2)], axis=0)
            for c in range(2)
        ],
        axis=1,
    ).astype(BF16)
    ordered = jnp.dot(stacked, perm_ref[...], preferred_element_type=F32)
    every = jnp.concatenate([ordered[16 * y : 16 * (y + 1)] for y in range(4)], axis=1)
    all_ref[...] = every
    half = half_ref[0]
    receivers = all_ref[:, pl.ds(pl.multiple_of(half * 512, 512), 512)]
    chosen = jnp.dot(every.astype(BF16), one_hot_ref[...], preferred_element_type=F32)
    even = iota(receivers.shape, 0) % 2 == 0
    turned = jnp.where(even, pltpu.roll(receivers, 15, 0), -pltpu.roll(receivers, 1, 0))
    chosen_t = chosen.T
    energy_src = jnp.sum(chosen_t * chosen_t, axis=1, keepdims=True)
    energy_rec = jnp.sum(receivers * receivers, axis=0, keepdims=True)
    scale = lax.rsqrt(jnp.maximum(energy_src * energy_rec, 1.0))
    left = chosen_t.astype(BF16)
    copies = []
    for part, right in enumerate((receivers, turned)):
        out_ref[part] = jnp.dot(left, right.astype(BF16), preferred_element_type=F32) * scale
        copies.append(pltpu.make_async_copy(out_ref.at[part], out_any.at[0, part], sems.at[part]))
        copies[-1].start()
    for copy in copies:
        copy.wait()


VMEM = pl.BlockSpec(memory_space=pltpu.VMEM)
SMEM = pl.BlockSpec(memory_space=pltpu.SMEM)
PARAMS = pltpu.CompilerParams(vmem_limit_bytes=32 * 1024 * 1024)


def prepare(conv_weight, in_weight, out_weight, sources, raw, flags):
    arrays = (
        conv_weight.transpose(0, 3, 4, 1, 2), in_weight.T, out_weight.reshape(1, F), sources.reshape(1, NV),
        raw, flags, jnp.asarray(sample_perm()), jnp.asarray(dft_table()), jnp.asarray(channel_perm()),
    )
    arrays = tuple(pltpu.with_memory_space_constraint(a, pltpu.HBM) for a in arrays)
    return pl.pallas_call(
        prepare_kernel,
        out_shape=(
            jax.ShapeDtypeStruct((LAYERS, BLK * F, 3 * 256), BF16),
            jax.ShapeDtypeStruct((EXT * F, 72), BF16),
            jax.ShapeDtypeStruct((OWN, OWN * F), BF16),
            jax.ShapeDtypeStruct((CH_ALL, NV), BF16),
        )
        + tuple(jax.ShapeDtypeStruct(a.shape, a.dtype) for a in arrays[4:]),
        in_specs=[pl.BlockSpec(memory_space=pl.ANY)] * 9,
        out_specs=(VMEM,) * 9,
        scratch_shapes=[pltpu.VMEM(a.shape, a.dtype) for a in arrays[:4]]
        + [pltpu.SemaphoreType.DMA((9,))],
        compiler_params=PARAMS,
        cost_estimate=pl.CostEstimate(flops=2_000_000, bytes_accessed=4_000_000, transcendentals=0),
        name="prepare",
    )(*arrays)


def denoise(edge, far, raw, near, flags, order, band, first, last, table):
    return pl.pallas_call(
        denoise_kernel,
        out_shape=jax.ShapeDtypeStruct((64, 128), BF16),
        in_specs=[SMEM] + [VMEM] * 9,
        out_specs=VMEM,
        scratch_shapes=[pltpu.VMEM(((EXT - 2 * i) * F, WIDE), BF16) for i in range(LAYERS + 1)]
        + [pltpu.VMEM((EXT * F, WIDE), BF16)] * 2
        + [pltpu.VMEM((64, 128), F32)],
        compiler_params=PARAMS,
        name="denoise",
    )(edge, far, raw, near, flags, order, band, first, last, table)


def turn(rows):
    return pl.pallas_call(
        turn_kernel,
        out_shape=jax.ShapeDtypeStruct((128, 128), BF16),
        in_specs=[VMEM],
        out_specs=VMEM,
        compiler_params=PARAMS,
        name="turn",
    )(rows)


def coherence(half, one_hot, perm, rows):
    return pl.pallas_call(
        coherence_kernel,
        out_shape=jax.ShapeDtypeStruct((1, 2, 128, 512), F32),
        in_specs=[SMEM, VMEM, VMEM, VMEM],
        out_specs=pl.BlockSpec(memory_space=pl.ANY),
        scratch_shapes=[
            pltpu.VMEM((16, CH_ALL), F32),
            pltpu.VMEM((2, 128, 512), F32),
            pltpu.SemaphoreType.DMA((2,)),
        ],
        compiler_params=PARAMS,
        name="coherence",
    )(half, one_hot, perm, rows)


CHAN = ("y", "z", "c")


def per_device(raw, flags, in_weight, conv_weight, out_weight, sources):
    count = lax.axis_size(CHAN)
    me = lax.axis_index(CHAN)
    odd = lax.axis_index("c")
    across = [(i, i + 1) for i in range(1, count - 1, 2)]
    near = lax.ppermute(raw, "c", [(0, 1), (1, 0)])
    far = lax.ppermute(raw, CHAN, across + [(b, a) for a, b in across])
    edge = jnp.stack([me == 0, me == count - 1, odd == 1]).astype(jnp.int32)
    half = lax.axis_index("w").reshape(1).astype(jnp.int32)
    band, first, last, one_hot, raw, flags, order, table, perm = prepare(
        conv_weight, in_weight, out_weight, sources, raw, flags
    )
    sent = denoise(edge, far, raw, near, flags, order, band, first, last, table)
    half, sent = lax.optimization_barrier((half, sent))
    got = lax.all_to_all(
        sent, "z", 0, 0, tiled=True, axis_index_groups=[[int(z) for z in Z_ORDER]]
    )
    rest = [((w * 2 + c) * 4 + y) * 2 + s for w in W_ORDER for c in range(2) for y in Y_ORDER for s in range(2)]
    mine = lax.all_to_all(turn(got), ("w", "c", "y", "s"), 0, 0, tiled=True, axis_index_groups=[rest])
    return coherence(half, one_hot, perm, mine)


def solution(mesh):
    fine = Mesh(mesh.devices.reshape(2, 4, 16, 2, 2), ("s", "y", "z", "c", "w"))
    placed = (P(("s", "w"), CHAN, None), P(("s", "w"), CHAN), P(), P(), P(), P())
    return jax.shard_map(
        per_device,
        mesh=fine,
        in_specs=placed,
        out_specs=P(("s",) + CHAN, None, None, "w"),
        check_vma=False,
    )
```

```python
import functools
import math

import jax
import jax.numpy as jnp
import numpy as np
from jax import lax
from jax.experimental import pallas as pl
from jax.experimental.pallas import tpu as pltpu
from jax.sharding import Mesh, PartitionSpec as P

NT = 640
F = 32
LAYERS = 3
NF = 256
OWN = 8
WIN = 2
EXT = OWN + 2 * LAYERS
BLK = 6
LANES = 128
PH = NT // LANES
CHUNK = WIN * LANES
WIDE = WIN * NT
CH_ALL = 1024
NV = 128
Y_ORDER = (2, 3, 0, 1)
W_ORDER = (1, 0)
Z_ORDER = tuple((np.arange(16) + 8) % 16)

water_level = 0.2
epsilon_power = 1e-06

F32 = jnp.float32
BF16 = jnp.bfloat16


def dft_table():
    part, z, core, y, section = np.meshgrid(
        np.arange(2), np.array(Z_ORDER), np.arange(2), np.array(Y_ORDER), np.arange(2), indexing="ij"
    )
    k = (section * 128 + (y * 16 + z) * 2 + core).reshape(-1)
    part = part.reshape(-1)
    phases = np.arange(NT)[:, None] * (k + 1)[None, :] % NT
    angles = phases.astype(np.float32) * np.float32(2.0 * math.pi / NT)
    table = np.where(part[None, :] == 0, np.cos(angles), -np.sin(angles))
    return table[sample_order()].astype(BF16)


def sample_order():
    return (np.arange(LANES)[None, :] * PH + np.arange(PH)[:, None]).reshape(-1)


def sample_perm():
    return np.eye(NT, dtype=np.float32)[:, sample_order()].astype(BF16)


def channel_perm():
    core, channel, z = np.meshgrid(np.arange(2), np.arange(OWN), np.array(Z_ORDER), indexing="ij")
    target = ((z * 2 + core) * OWN + channel).reshape(-1)
    return np.eye(256, dtype=np.float32)[target].astype(BF16)


def iota(shape, dim):
    return lax.broadcasted_iota(jnp.int32, shape, dim)


def column(row, n):
    eye = iota((n, n), 0) == iota((n, n), 1)
    return jnp.sum(jnp.where(eye, jnp.broadcast_to(row, (n, n)), 0.0), axis=1, keepdims=True)


def swap_bits(x, row_step, lane_step):
    rows, lanes = x.shape
    row_bit = (iota(x.shape, 0) // row_step) % 2
    lane_bit = (iota(x.shape, 1) // lane_step) % 2
    down = pltpu.roll(pltpu.roll(x, rows - row_step, 0), lane_step, 1)
    up = pltpu.roll(pltpu.roll(x, row_step, 0), lanes - lane_step, 1)
    return jnp.where(row_bit == lane_bit, x, jnp.where(row_bit == 0, down, up))


def pack_kernel(raw_any, flags_any, own_ref, flags_ref, sems):
    copies = (
        pltpu.make_async_copy(flags_any, flags_ref, sems.at[0]),
        pltpu.make_async_copy(raw_any, own_ref.at[:, :, pl.ds(0, NT)], sems.at[1]),
    )
    for copy in copies:
        copy.start()
    copies[0].wait()
    for w in range(WIN):
        flags = column(flags_ref[w : w + 1, :].astype(F32), OWN)
        own_ref[w, :, NT:] = jnp.broadcast_to(flags, (OWN, LANES)).astype(BF16)
    copies[1].wait()


def prepare_kernel(
    cut_ref, conv_any, in_any, out_any, sources_any, order_any, table_any, perm_any,
    band_ref, first_ref, last_ref, one_hot_ref, order_ref, table_ref, perm_ref,
    conv_ref, in_ref, out_ref, sources_ref, sems,
):
    pairs = (
        (conv_any, conv_ref), (in_any, in_ref), (out_any, out_ref), (sources_any, sources_ref),
        (order_any, order_ref), (table_any, table_ref), (perm_any, perm_ref),
    )
    copies = [pltpu.make_async_copy(a, b, sems.at[i]) for i, (a, b) in enumerate(pairs)]
    for copy in copies:
        copy.start()
    copies[1].wait()
    shape = (EXT * F, 48)
    channel = iota(shape, 0) // F
    place = jnp.where(channel < 7, OWN + 1 + channel, channel - 7)
    lane = iota(shape, 1)
    first = jnp.zeros(shape, F32)
    for tap in range(3):
        weight = column(in_ref[tap : tap + 1, :].astype(F32), F)
        tall = jnp.broadcast_to(jnp.concatenate([weight] * EXT, axis=0), shape)
        first = jnp.where(lane == place + 16 * tap, tall, first)
    first_ref[...] = first.astype(BF16)
    copies[2].wait()
    shape = (OWN, OWN * F)
    wide = jnp.concatenate([out_ref[...].astype(F32)] * OWN, axis=1)
    last_ref[...] = jnp.where(
        iota(shape, 0) == iota(shape, 1) // F, jnp.broadcast_to(wide, shape), 0.0
    ).astype(BF16)
    copies[3].wait()
    shape = (CH_ALL, NV)
    j = (sources_ref[...] + OWN // 2) % CH_ALL
    z = ((j // 16) % 16 - Z_ORDER[0]) % 16
    row = (j // 256) * 256 + ((j // 8) % 2) * 128 + (j % 8) * 16 + z
    one_hot_ref[...] = jnp.where(iota(shape, 0) == jnp.broadcast_to(row, shape), 1.0, 0.0).astype(BF16)
    copies[0].wait()
    for layer in range(LAYERS):
        for tap in range(3):
            taps = [conv_ref[layer, a, tap] for a in range(3)]
            base = jnp.concatenate(taps + [jnp.zeros((F, 256 - 3 * F), BF16)], axis=1)
            for c in range(BLK):
                row = base if c == 0 else pltpu.roll(base, F * c, 1)
                for block in range(2):
                    band_ref[layer, block, F * c : F * (c + 1), 256 * tap : 256 * (tap + 1)] = row

    @pl.when(cut_ref[0] == 1)
    def _():
        for layer in range(LAYERS):
            for block in range(2):
                start = block * (EXT - 2 * (layer + 1) - BLK) + layer
                for c, k in ((5 - start, 7 - start), (6 - start, 6 - start)):
                    if 0 <= c < BLK:
                        for tap in range(3):
                            lanes = slice(256 * tap + F * k, 256 * tap + F * (k + 1))
                            band_ref[layer, block, F * c : F * (c + 1), lanes] = jnp.zeros((F, F), BF16)

    for copy in copies[4:]:
        copy.wait()


def lane_shift(x, step):
    edge = iota((x.shape[0], LANES), 1) == (0 if step == 1 else LANES - 1)
    moved = [
        jnp.where(edge, jnp.zeros_like(part), pltpu.roll(part, step % LANES, 1))
        for part in (x[:, i : i + LANES] for i in range(0, x.shape[1], LANES))
    ]
    return jnp.concatenate(moved, axis=1)


def denoise_kernel(
    own_ref, left_ref, order_ref, band_ref, first_ref, last_ref, table_ref,
    out_ref, h0_ref, h1_ref, h2_ref, h3_ref, earlier_ref, later_ref, line_ref,
):
    rows = [ref[w, :, :NT].astype(F32) for w in range(WIN) for ref in (own_ref, left_ref)]
    rows = jnp.concatenate(rows, axis=0).astype(BF16)
    rows = jnp.dot(rows, order_ref[...], preferred_element_type=F32)
    lines = [
        jnp.concatenate(
            [rows[16 * w : 16 * (w + 1), v * LANES : (v + 1) * LANES] for w in range(WIN)], axis=1
        )
        for v in range(PH)
    ]
    hidden = (h0_ref, h1_ref, h2_ref, h3_ref)
    chunk = [slice(v * CHUNK, (v + 1) * CHUNK) for v in range(PH)]
    for v in range(PH):
        before = lines[v - 1] if v > 0 else lane_shift(lines[PH - 1], 1)
        after = lines[v + 1] if v < PH - 1 else lane_shift(lines[0], -1)
        taps = jnp.concatenate([before, lines[v], after], axis=0).astype(BF16)
        h0_ref[:, chunk[v]] = jnp.dot(first_ref[...], taps, preferred_element_type=F32).astype(BF16)
    spectra = None
    for layer in range(LAYERS):
        step = 2**layer
        source, target = hidden[layer], hidden[layer + 1]
        size = (EXT - 2 * layer) * F
        count = EXT - 2 * (layer + 1)
        for v in sorted(range(PH), key=lambda v: (v < step) + (v >= PH - step)):
            before, after, u, t = source, source, v - step, v + step
            if u < 0:
                u += PH
                before = earlier_ref
                earlier_ref[:size, chunk[u]] = lane_shift(source[:, chunk[u]], 1)
            if t >= PH:
                t -= PH
                after = later_ref
                later_ref[:size, chunk[t]] = lane_shift(source[:, chunk[t]], -1)
            for block, start, low in ((0, 0, 0), (1, count - BLK, 2 * BLK - count)):
                k = slice(start * F, (start + BLK + 2) * F)
                taps = jnp.concatenate([before[k, chunk[u]], source[k, chunk[v]], after[k, chunk[t]]], axis=0)
                total = jnp.dot(band_ref[layer, block, low * F :, :], taps, preferred_element_type=F32)
                old = source[(start + low + 1) * F : (start + BLK + 1) * F, chunk[v]].astype(F32)
                new = old + jnp.maximum(total, 0.0)
                target[(start + low) * F : (start + BLK) * F, chunk[v]] = new.astype(BF16)
            if layer == LAYERS - 1:
                clean = jnp.dot(last_ref[...], target[:, chunk[v]], preferred_element_type=F32)
                clean = jnp.concatenate([clean[:, :LANES], clean[:, LANES:]], axis=0).astype(BF16)
                term = jnp.dot(clean, table_ref[v * LANES : (v + 1) * LANES, :], preferred_element_type=F32)
                spectra = term if spectra is None else spectra + term
    real, imag = spectra[:, :NF], spectra[:, NF:]
    power = real * real + imag * imag
    spread = jnp.sqrt(jnp.mean(power, axis=1, keepdims=True) + epsilon_power)
    flags = jnp.concatenate(
        [
            ref[w, :, NT : NT + 1].astype(F32)[part]
            for w in range(WIN)
            for ref, part in ((left_ref, slice(4, 8)), (own_ref, slice(0, 4)))
        ],
        axis=0,
    )
    factor = flags / (jnp.sqrt(power) + water_level * spread)
    for part, value in enumerate((real * factor, imag * factor)):
        for w in range(WIN):
            for high in range(2):
                x = value[w * OWN : (w + 1) * OWN, high * 128 : (high + 1) * 128]
                for bit in range(3):
                    x = swap_bits(x, 2**bit, 16 * 2**bit)
                line_ref[pl.ds(32 * high + 2 * w + part, 8, stride=4), :] = x
    out_ref[...] = line_ref[...].astype(BF16)


def turn_kernel(in_ref, out_ref):
    x = in_ref[...].astype(F32)
    for bit in range(4):
        x = swap_bits(x, 4 * 2**bit, 2**bit)
    x = x.astype(BF16)
    out_ref[:64, :] = x
    out_ref[64:, :] = x


def coherence_kernel(half_ref, one_hot_ref, perm_ref, in_ref, out_any, all_ref, out_ref, sems):
    x = in_ref[...].astype(F32)

    def piece(w, c, y):
        start = ((w * 2 + c) * 4 + Y_ORDER.index(y)) * 8
        return x[start : start + 8]

    stacked = jnp.concatenate(
        [
            jnp.concatenate([piece(w, c, y) for y in range(4) for w in range(2)], axis=0)
            for c in range(2)
        ],
        axis=1,
    ).astype(BF16)
    ordered = jnp.dot(stacked, perm_ref[...], preferred_element_type=F32)
    every = jnp.concatenate([ordered[16 * y : 16 * (y + 1)] for y in range(4)], axis=1)
    all_ref[...] = pltpu.roll(every, CH_ALL - OWN // 2, 1)
    half = half_ref[0]
    receivers = all_ref[:, pl.ds(pl.multiple_of(half * 512, 512), 512)]
    gathered = jnp.concatenate([stacked[16 * y : 16 * (y + 1)] for y in range(4)], axis=1)
    chosen = jnp.dot(gathered, one_hot_ref[...], preferred_element_type=F32)
    even = iota(receivers.shape, 0) % 2 == 0
    turned = jnp.where(even, pltpu.roll(receivers, 15, 0), -pltpu.roll(receivers, 1, 0))
    chosen_t = chosen.T
    energy_src = jnp.sum(chosen_t * chosen_t, axis=1, keepdims=True)
    energy_rec = jnp.sum(receivers * receivers, axis=0, keepdims=True)
    scale = lax.rsqrt(jnp.maximum(energy_src * energy_rec, 1.0))
    left = chosen_t.astype(BF16)
    copies = []
    for part, right in enumerate((receivers, turned)):
        out_ref[part] = jnp.dot(left, right.astype(BF16), preferred_element_type=F32) * scale
        copies.append(pltpu.make_async_copy(out_ref.at[part], out_any.at[0, part], sems.at[part]))
        copies[-1].start()
    for copy in copies:
        copy.wait()


VMEM = pl.BlockSpec(memory_space=pltpu.VMEM)
SMEM = pl.BlockSpec(memory_space=pltpu.SMEM)
PARAMS = pltpu.CompilerParams(vmem_limit_bytes=32 * 1024 * 1024)


def pack(raw, flags):
    raw, flags = (pltpu.with_memory_space_constraint(a, pltpu.HBM) for a in (raw, flags))
    return pl.pallas_call(
        pack_kernel,
        out_shape=jax.ShapeDtypeStruct((WIN, OWN, NT + LANES), BF16),
        in_specs=[pl.BlockSpec(memory_space=pl.ANY)] * 2,
        out_specs=VMEM,
        scratch_shapes=[pltpu.VMEM(flags.shape, flags.dtype), pltpu.SemaphoreType.DMA((2,))],
        compiler_params=PARAMS,
        name="pack",
    )(raw, flags)


def prepare(cut, conv_weight, in_weight, out_weight, sources):
    arrays = (
        conv_weight.transpose(0, 3, 4, 1, 2), in_weight.T, out_weight.reshape(1, F), sources.reshape(1, NV),
        jnp.asarray(sample_perm()), jnp.asarray(dft_table()), jnp.asarray(channel_perm()),
    )
    arrays = tuple(pltpu.with_memory_space_constraint(a, pltpu.HBM) for a in arrays)
    return pl.pallas_call(
        prepare_kernel,
        out_shape=(
            jax.ShapeDtypeStruct((LAYERS, 2, BLK * F, 3 * 256), BF16),
            jax.ShapeDtypeStruct((EXT * F, 48), BF16),
            jax.ShapeDtypeStruct((OWN, OWN * F), BF16),
            jax.ShapeDtypeStruct((CH_ALL, NV), BF16),
        )
        + tuple(jax.ShapeDtypeStruct(a.shape, a.dtype) for a in arrays[4:]),
        in_specs=[SMEM] + [pl.BlockSpec(memory_space=pl.ANY)] * 7,
        out_specs=(VMEM,) * 7,
        scratch_shapes=[pltpu.VMEM(a.shape, a.dtype) for a in arrays[:4]]
        + [pltpu.SemaphoreType.DMA((7,))],
        compiler_params=PARAMS,
        cost_estimate=pl.CostEstimate(flops=2_000_000, bytes_accessed=4_000_000, transcendentals=0),
        name="prepare",
    )(cut, *arrays)


def denoise(own, left, order, band, first, last, table):
    return pl.pallas_call(
        denoise_kernel,
        out_shape=jax.ShapeDtypeStruct((64, 128), BF16),
        in_specs=[VMEM] * 7,
        out_specs=VMEM,
        scratch_shapes=[pltpu.VMEM(((EXT - 2 * i) * F, WIDE), BF16) for i in range(LAYERS + 1)]
        + [pltpu.VMEM((EXT * F, WIDE), BF16)] * 2
        + [pltpu.VMEM((64, 128), F32)],
        compiler_params=PARAMS,
        name="denoise",
    )(own, left, order, band, first, last, table)


def turn(rows):
    return pl.pallas_call(
        turn_kernel,
        out_shape=jax.ShapeDtypeStruct((128, 128), BF16),
        in_specs=[VMEM],
        out_specs=VMEM,
        compiler_params=PARAMS,
        name="turn",
    )(rows)


def coherence(half, one_hot, perm, rows):
    return pl.pallas_call(
        coherence_kernel,
        out_shape=jax.ShapeDtypeStruct((1, 2, 128, 512), F32),
        in_specs=[SMEM, VMEM, VMEM, VMEM],
        out_specs=pl.BlockSpec(memory_space=pl.ANY),
        scratch_shapes=[
            pltpu.VMEM((16, CH_ALL), F32),
            pltpu.VMEM((2, 128, 512), F32),
            pltpu.SemaphoreType.DMA((2,)),
        ],
        compiler_params=PARAMS,
        name="coherence",
    )(half, one_hot, perm, rows)


CHAN = ("y", "z", "c")


def per_device(raw, flags, in_weight, conv_weight, out_weight, sources):
    count = lax.axis_size(CHAN)
    own = pack(raw, flags)
    left = lax.ppermute(own, CHAN, [(i, (i + 1) % count) for i in range(count)])
    cut = (lax.axis_index(CHAN) == 0).astype(jnp.int32).reshape(1)
    half = lax.axis_index("w").reshape(1).astype(jnp.int32)
    band, first, last, one_hot, order, table, perm = prepare(cut, conv_weight, in_weight, out_weight, sources)
    sent = denoise(own, left, order, band, first, last, table)
    half, sent = lax.optimization_barrier((half, sent))
    got = lax.all_to_all(
        sent, "z", 0, 0, tiled=True, axis_index_groups=[[int(z) for z in Z_ORDER]]
    )
    rest = [((w * 2 + c) * 4 + y) * 2 + s for w in W_ORDER for c in range(2) for y in Y_ORDER for s in range(2)]
    mine = lax.all_to_all(turn(got), ("w", "c", "y", "s"), 0, 0, tiled=True, axis_index_groups=[rest])
    return coherence(half, one_hot, perm, mine)


def solution(mesh):
    fine = Mesh(mesh.devices.reshape(2, 4, 16, 2, 2), ("s", "y", "z", "c", "w"))
    placed = (P(("s", "w"), CHAN, None), P(("s", "w"), CHAN), P(), P(), P(), P())
    return jax.shard_map(
        per_device,
        mesh=fine,
        in_specs=placed,
        out_specs=P(("s",) + CHAN, None, None, "w"),
        check_vma=False,
    )
```

```python
import functools
import math

import jax
import jax.numpy as jnp
import numpy as np
from jax import lax
from jax.experimental import pallas as pl
from jax.experimental.pallas import tpu as pltpu
from jax.sharding import Mesh, PartitionSpec as P

NT = 640
F = 32
LAYERS = 3
NF = 256
OWN = 8
WIN = 2
EXT = OWN + 2 * LAYERS
BLK = 6
LANES = 128
PH = NT // LANES
CHUNK = WIN * LANES
WIDE = WIN * NT
CH_ALL = 1024
NV = 128
Y_ORDER = (2, 3, 0, 1)
W_ORDER = (1, 0)
Z_ORDER = tuple((np.arange(16) + 8) % 16)

water_level = 0.2
epsilon_power = 1e-06

F32 = jnp.float32
BF16 = jnp.bfloat16


def dft_table():
    part, z, core, y, section = np.meshgrid(
        np.arange(2), np.array(Z_ORDER), np.arange(2), np.array(Y_ORDER), np.arange(2), indexing="ij"
    )
    k = (section * 128 + (y * 16 + z) * 2 + core).reshape(-1)
    part = part.reshape(-1)
    phases = np.arange(NT)[:, None] * (k + 1)[None, :] % NT
    angles = phases.astype(np.float32) * np.float32(2.0 * math.pi / NT)
    table = np.where(part[None, :] == 0, np.cos(angles), -np.sin(angles))
    return table[sample_order()].astype(BF16)


def sample_order():
    return (np.arange(LANES)[None, :] * PH + np.arange(PH)[:, None]).reshape(-1)


def sample_perm():
    return np.eye(NT, dtype=np.float32)[:, sample_order()].astype(BF16)


def channel_perm():
    core, channel, z = np.meshgrid(np.arange(2), np.arange(OWN), np.array(Z_ORDER), indexing="ij")
    target = ((z * 2 + core) * OWN + channel).reshape(-1)
    return np.eye(256, dtype=np.float32)[target].astype(BF16)


def iota(shape, dim):
    return lax.broadcasted_iota(jnp.int32, shape, dim)


def column(row, n):
    eye = iota((n, n), 0) == iota((n, n), 1)
    return jnp.sum(jnp.where(eye, jnp.broadcast_to(row, (n, n)), 0.0), axis=1, keepdims=True)


def swap_bits(x, row_step, lane_step):
    rows, lanes = x.shape
    row_bit = (iota(x.shape, 0) // row_step) % 2
    lane_bit = (iota(x.shape, 1) // lane_step) % 2
    down = pltpu.roll(pltpu.roll(x, rows - row_step, 0), lane_step, 1)
    up = pltpu.roll(pltpu.roll(x, row_step, 0), lanes - lane_step, 1)
    return jnp.where(row_bit == lane_bit, x, jnp.where(row_bit == 0, down, up))


def pack_kernel(raw_any, flags_any, own_ref, flags_ref, sems):
    copies = (
        pltpu.make_async_copy(flags_any, flags_ref, sems.at[0]),
        pltpu.make_async_copy(raw_any, own_ref.at[:, :, pl.ds(0, NT)], sems.at[1]),
    )
    for copy in copies:
        copy.start()
    copies[0].wait()
    for w in range(WIN):
        flags = column(flags_ref[w : w + 1, :].astype(F32), OWN)
        own_ref[w, :, NT:] = jnp.broadcast_to(flags, (OWN, LANES)).astype(BF16)
    copies[1].wait()


def prepare_kernel(
    cut_ref, conv_any, in_any, out_any, sources_any, order_any, table_any, perm_any,
    band_ref, first_ref, last_ref, one_hot_ref, order_ref, table_ref, perm_ref,
    conv_ref, in_ref, out_ref, sources_ref, sems,
):
    pairs = (
        (conv_any, conv_ref), (in_any, in_ref), (out_any, out_ref), (sources_any, sources_ref),
        (order_any, order_ref), (table_any, table_ref), (perm_any, perm_ref),
    )
    copies = [pltpu.make_async_copy(a, b, sems.at[i]) for i, (a, b) in enumerate(pairs)]
    for copy in copies:
        copy.start()
    copies[1].wait()
    shape = (EXT * F, 48)
    channel = iota(shape, 0) // F
    place = jnp.where(channel < 7, OWN + 1 + channel, channel - 7)
    lane = iota(shape, 1)
    first = jnp.zeros(shape, F32)
    for tap in range(3):
        weight = column(in_ref[tap : tap + 1, :].astype(F32), F)
        tall = jnp.broadcast_to(jnp.concatenate([weight] * EXT, axis=0), shape)
        first = jnp.where(lane == place + 16 * tap, tall, first)
    first_ref[...] = first.astype(BF16)
    copies[2].wait()
    shape = (OWN, OWN * F)
    wide = jnp.concatenate([out_ref[...].astype(F32)] * OWN, axis=1)
    last_ref[...] = jnp.where(
        iota(shape, 0) == iota(shape, 1) // F, jnp.broadcast_to(wide, shape), 0.0
    ).astype(BF16)
    copies[3].wait()
    shape = (CH_ALL, NV)
    j = (sources_ref[...] + CH_ALL - OWN // 2) % CH_ALL
    z = ((j // 16) % 16 - Z_ORDER[0]) % 16
    row = (j // 256) * 256 + ((j // 8) % 2) * 128 + (j % 8) * 16 + z
    one_hot_ref[...] = jnp.where(iota(shape, 0) == jnp.broadcast_to(row, shape), 1.0, 0.0).astype(BF16)
    copies[0].wait()
    for layer in range(LAYERS):
        for tap in range(3):
            taps = [conv_ref[layer, a, tap] for a in range(3)]
            base = jnp.concatenate(taps + [jnp.zeros((F, 256 - 3 * F), BF16)], axis=1)
            for c in range(BLK):
                row = base if c == 0 else pltpu.roll(base, F * c, 1)
                for block in range(2):
                    band_ref[layer, block, F * c : F * (c + 1), 256 * tap : 256 * (tap + 1)] = row

    @pl.when(cut_ref[0] == 1)
    def _():
        for layer in range(LAYERS):
            for block in range(2):
                start = block * (EXT - 2 * (layer + 1) - BLK) + layer
                for c, k in ((5 - start, 7 - start), (6 - start, 6 - start)):
                    if 0 <= c < BLK:
                        for tap in range(3):
                            lanes = slice(256 * tap + F * k, 256 * tap + F * (k + 1))
                            band_ref[layer, block, F * c : F * (c + 1), lanes] = jnp.zeros((F, F), BF16)

    for copy in copies[4:]:
        copy.wait()


def lane_shift(x, step):
    edge = iota((x.shape[0], LANES), 1) == (0 if step == 1 else LANES - 1)
    moved = [
        jnp.where(edge, jnp.zeros_like(part), pltpu.roll(part, step % LANES, 1))
        for part in (x[:, i : i + LANES] for i in range(0, x.shape[1], LANES))
    ]
    return jnp.concatenate(moved, axis=1)


def denoise_kernel(
    after_ref, own_ref, order_ref, band_ref, first_ref, last_ref, table_ref,
    out_ref, h0_ref, h1_ref, h2_ref, h3_ref, earlier_ref, later_ref, line_ref,
):
    rows = [ref[w, :, :NT].astype(F32) for w in range(WIN) for ref in (after_ref, own_ref)]
    rows = jnp.concatenate(rows, axis=0).astype(BF16)
    rows = jnp.dot(rows, order_ref[...], preferred_element_type=F32)
    lines = [
        jnp.concatenate(
            [rows[16 * w : 16 * (w + 1), v * LANES : (v + 1) * LANES] for w in range(WIN)], axis=1
        )
        for v in range(PH)
    ]
    hidden = (h0_ref, h1_ref, h2_ref, h3_ref)
    chunk = [slice(v * CHUNK, (v + 1) * CHUNK) for v in range(PH)]
    for v in range(PH):
        before = lines[v - 1] if v > 0 else lane_shift(lines[PH - 1], 1)
        after = lines[v + 1] if v < PH - 1 else lane_shift(lines[0], -1)
        taps = jnp.concatenate([before, lines[v], after], axis=0).astype(BF16)
        h0_ref[:, chunk[v]] = jnp.dot(first_ref[...], taps, preferred_element_type=F32).astype(BF16)
    for layer in range(LAYERS):
        step = 2**layer
        source, target = hidden[layer], hidden[layer + 1]
        size = (EXT - 2 * layer) * F
        count = EXT - 2 * (layer + 1)
        for v in sorted(range(PH), key=lambda v: (v < step) + (v >= PH - step)):
            before, after, u, t = source, source, v - step, v + step
            if u < 0:
                u += PH
                before = earlier_ref
                earlier_ref[:size, chunk[u]] = lane_shift(source[:, chunk[u]], 1)
            if t >= PH:
                t -= PH
                after = later_ref
                later_ref[:size, chunk[t]] = lane_shift(source[:, chunk[t]], -1)
            for block, start, low in ((0, 0, 0), (1, count - BLK, 2 * BLK - count)):
                k = slice(start * F, (start + BLK + 2) * F)
                taps = jnp.concatenate([before[k, chunk[u]], source[k, chunk[v]], after[k, chunk[t]]], axis=0)
                total = jnp.dot(band_ref[layer, block, low * F :, :], taps, preferred_element_type=F32)
                old = source[(start + low + 1) * F : (start + BLK + 1) * F, chunk[v]].astype(F32)
                new = old + jnp.maximum(total, 0.0)
                for i in range(BLK - low):
                    c = start + low + i
                    target[c * F : (c + 1) * F, chunk[v]] = new[i * F : (i + 1) * F].astype(BF16)
    clean = jnp.dot(last_ref[...], h3_ref[...], preferred_element_type=F32)
    clean = jnp.concatenate(
        [
            jnp.concatenate(
                [clean[:, v * CHUNK + w * LANES : v * CHUNK + (w + 1) * LANES] for v in range(PH)], axis=1
            )
            for w in range(WIN)
        ],
        axis=0,
    )
    spectra = jnp.dot(clean.astype(BF16), table_ref[...], preferred_element_type=F32)
    real, imag = spectra[:, :NF], spectra[:, NF:]
    power = real * real + imag * imag
    spread = jnp.sqrt(jnp.mean(power, axis=1, keepdims=True) + epsilon_power)
    flags = jnp.concatenate(
        [
            ref[w, :, NT : NT + 1].astype(F32)[part]
            for w in range(WIN)
            for ref, part in ((own_ref, slice(4, 8)), (after_ref, slice(0, 4)))
        ],
        axis=0,
    )
    factor = flags / (jnp.sqrt(power) + water_level * spread)
    for part, value in enumerate((real * factor, imag * factor)):
        for w in range(WIN):
            for high in range(2):
                x = value[w * OWN : (w + 1) * OWN, high * 128 : (high + 1) * 128]
                for bit in range(3):
                    x = swap_bits(x, 2**bit, 16 * 2**bit)
                line_ref[pl.ds(32 * high + 2 * w + part, 8, stride=4), :] = x
    out_ref[...] = line_ref[...].astype(BF16)


def turn_kernel(in_ref, out_ref):
    x = in_ref[...].astype(F32)
    for bit in range(4):
        x = swap_bits(x, 4 * 2**bit, 2**bit)
    x = x.astype(BF16)
    out_ref[:64, :] = x
    out_ref[64:, :] = x


def coherence_kernel(half_ref, one_hot_ref, perm_ref, in_ref, out_any, all_ref, out_ref, sems):
    x = in_ref[...].astype(F32)

    def piece(w, c, y):
        start = ((w * 2 + c) * 4 + Y_ORDER.index(y)) * 8
        return x[start : start + 8]

    stacked = jnp.concatenate(
        [
            jnp.concatenate([piece(w, c, y) for y in range(4) for w in range(2)], axis=0)
            for c in range(2)
        ],
        axis=1,
    ).astype(BF16)
    ordered = jnp.dot(stacked, perm_ref[...], preferred_element_type=F32)
    every = jnp.concatenate([ordered[16 * y : 16 * (y + 1)] for y in range(4)], axis=1)
    all_ref[...] = pltpu.roll(every, OWN // 2, 1)
    half = half_ref[0]
    receivers = all_ref[:, pl.ds(pl.multiple_of(half * 512, 512), 512)]
    gathered = jnp.concatenate([stacked[16 * y : 16 * (y + 1)] for y in range(4)], axis=1)
    chosen = jnp.dot(gathered, one_hot_ref[...], preferred_element_type=F32)
    even = iota(receivers.shape, 0) % 2 == 0
    turned = jnp.where(even, pltpu.roll(receivers, 15, 0), -pltpu.roll(receivers, 1, 0))
    chosen_t = chosen.T
    energy_src = jnp.sum(chosen_t * chosen_t, axis=1, keepdims=True)
    energy_rec = jnp.sum(receivers * receivers, axis=0, keepdims=True)
    scale = lax.rsqrt(jnp.maximum(energy_src * energy_rec, 1.0))
    left = chosen_t.astype(BF16)
    copies = []
    for part, right in enumerate((receivers, turned)):
        out_ref[part] = jnp.dot(left, right.astype(BF16), preferred_element_type=F32) * scale
        copies.append(pltpu.make_async_copy(out_ref.at[part], out_any.at[0, part], sems.at[part]))
        copies[-1].start()
    for copy in copies:
        copy.wait()


VMEM = pl.BlockSpec(memory_space=pltpu.VMEM)
SMEM = pl.BlockSpec(memory_space=pltpu.SMEM)
PARAMS = pltpu.CompilerParams(vmem_limit_bytes=32 * 1024 * 1024)


def pack(raw, flags):
    raw, flags = (pltpu.with_memory_space_constraint(a, pltpu.HBM) for a in (raw, flags))
    return pl.pallas_call(
        pack_kernel,
        out_shape=jax.ShapeDtypeStruct((WIN, OWN, NT + LANES), BF16),
        in_specs=[pl.BlockSpec(memory_space=pl.ANY)] * 2,
        out_specs=VMEM,
        scratch_shapes=[pltpu.VMEM(flags.shape, flags.dtype), pltpu.SemaphoreType.DMA((2,))],
        compiler_params=PARAMS,
        name="pack",
    )(raw, flags)


def prepare(cut, conv_weight, in_weight, out_weight, sources):
    arrays = (
        conv_weight.transpose(0, 3, 4, 1, 2), in_weight.T, out_weight.reshape(1, F), sources.reshape(1, NV),
        jnp.asarray(sample_perm()), jnp.asarray(dft_table()), jnp.asarray(channel_perm()),
    )
    arrays = tuple(pltpu.with_memory_space_constraint(a, pltpu.HBM) for a in arrays)
    return pl.pallas_call(
        prepare_kernel,
        out_shape=(
            jax.ShapeDtypeStruct((LAYERS, 2, BLK * F, 3 * 256), BF16),
            jax.ShapeDtypeStruct((EXT * F, 48), BF16),
            jax.ShapeDtypeStruct((OWN, OWN * F), BF16),
            jax.ShapeDtypeStruct((CH_ALL, NV), BF16),
        )
        + tuple(jax.ShapeDtypeStruct(a.shape, a.dtype) for a in arrays[4:]),
        in_specs=[SMEM] + [pl.BlockSpec(memory_space=pl.ANY)] * 7,
        out_specs=(VMEM,) * 7,
        scratch_shapes=[pltpu.VMEM(a.shape, a.dtype) for a in arrays[:4]]
        + [pltpu.SemaphoreType.DMA((7,))],
        compiler_params=PARAMS,
        cost_estimate=pl.CostEstimate(flops=2_000_000, bytes_accessed=4_000_000, transcendentals=0),
        name="prepare",
    )(cut, *arrays)


def denoise(after, own, order, band, first, last, table):
    return pl.pallas_call(
        denoise_kernel,
        out_shape=jax.ShapeDtypeStruct((64, 128), BF16),
        in_specs=[VMEM] * 7,
        out_specs=VMEM,
        scratch_shapes=[pltpu.VMEM(((EXT - 2 * i) * F, WIDE), BF16) for i in range(LAYERS + 1)]
        + [pltpu.VMEM((EXT * F, WIDE), BF16)] * 2
        + [pltpu.VMEM((64, 128), F32)],
        compiler_params=PARAMS,
        name="denoise",
    )(after, own, order, band, first, last, table)


def turn(rows):
    return pl.pallas_call(
        turn_kernel,
        out_shape=jax.ShapeDtypeStruct((128, 128), BF16),
        in_specs=[VMEM],
        out_specs=VMEM,
        compiler_params=PARAMS,
        name="turn",
    )(rows)


def coherence(half, one_hot, perm, rows):
    return pl.pallas_call(
        coherence_kernel,
        out_shape=jax.ShapeDtypeStruct((1, 2, 128, 512), F32),
        in_specs=[SMEM, VMEM, VMEM, VMEM],
        out_specs=pl.BlockSpec(memory_space=pl.ANY),
        scratch_shapes=[
            pltpu.VMEM((16, CH_ALL), F32),
            pltpu.VMEM((2, 128, 512), F32),
            pltpu.SemaphoreType.DMA((2,)),
        ],
        compiler_params=PARAMS,
        name="coherence",
    )(half, one_hot, perm, rows)


CHAN = ("y", "z", "c")


def per_device(raw, flags, in_weight, conv_weight, out_weight, sources):
    count = lax.axis_size(CHAN)
    own = pack(raw, flags)
    after = lax.ppermute(own, CHAN, [((i + 1) % count, i) for i in range(count)])
    cut = (lax.axis_index(CHAN) == count - 1).astype(jnp.int32).reshape(1)
    half = lax.axis_index("w").reshape(1).astype(jnp.int32)
    band, first, last, one_hot, order, table, perm = prepare(cut, conv_weight, in_weight, out_weight, sources)
    sent = denoise(after, own, order, band, first, last, table)
    half, sent = lax.optimization_barrier((half, sent))
    got = lax.all_to_all(
        sent, "z", 0, 0, tiled=True, axis_index_groups=[[int(z) for z in Z_ORDER]]
    )
    rest = [((w * 2 + c) * 4 + y) * 2 + s for w in W_ORDER for c in range(2) for y in Y_ORDER for s in range(2)]
    mine = lax.all_to_all(turn(got), ("w", "c", "y", "s"), 0, 0, tiled=True, axis_index_groups=[rest])
    return coherence(half, one_hot, perm, mine)


def solution(mesh):
    fine = Mesh(mesh.devices.reshape(2, 4, 16, 2, 2), ("s", "y", "z", "c", "w"))
    placed = (P(("s", "w"), CHAN, None), P(("s", "w"), CHAN), P(), P(), P(), P())
    return jax.shard_map(
        per_device,
        mesh=fine,
        in_specs=placed,
        out_specs=P(("s",) + CHAN, None, None, "w"),
        check_vma=False,
    )
```

```python
import functools
import math

import jax
import jax.numpy as jnp
import numpy as np
from jax import lax
from jax.experimental import pallas as pl
from jax.experimental.pallas import tpu as pltpu
from jax.sharding import Mesh, PartitionSpec as P

NT = 640
F = 32
LAYERS = 3
NF = 256
OWN = 8
WIN = 2
EXT = OWN + 2 * LAYERS
BLK = 6
LANES = 128
PH = NT // LANES
CHUNK = WIN * LANES
WIDE = WIN * NT
CH_ALL = 1024
NV = 128
Y_ORDER = (2, 3, 0, 1)
W_ORDER = (1, 0)
Z_ORDER = tuple((np.arange(16) + 8) % 16)

water_level = 0.2
epsilon_power = 1e-06

F32 = jnp.float32
BF16 = jnp.bfloat16


def dft_table():
    part, z, core, y, section = np.meshgrid(
        np.arange(2), np.array(Z_ORDER), np.arange(2), np.array(Y_ORDER), np.arange(2), indexing="ij"
    )
    k = (section * 128 + (y * 16 + z) * 2 + core).reshape(-1)
    part = part.reshape(-1)
    phases = np.arange(NT)[:, None] * (k + 1)[None, :] % NT
    angles = phases.astype(np.float32) * np.float32(2.0 * math.pi / NT)
    table = np.where(part[None, :] == 0, np.cos(angles), -np.sin(angles))
    return table[sample_order()].astype(BF16)


def sample_order():
    return (np.arange(LANES)[None, :] * PH + np.arange(PH)[:, None]).reshape(-1)


def sample_perm():
    return np.eye(NT, dtype=np.float32)[:, sample_order()].astype(BF16)


def channel_perm():
    core, channel, z = np.meshgrid(np.arange(2), np.arange(OWN), np.array(Z_ORDER), indexing="ij")
    target = ((z * 2 + core) * OWN + channel).reshape(-1)
    return np.eye(256, dtype=np.float32)[target].astype(BF16)


def iota(shape, dim):
    return lax.broadcasted_iota(jnp.int32, shape, dim)


def column(row, n):
    eye = iota((n, n), 0) == iota((n, n), 1)
    return jnp.sum(jnp.where(eye, jnp.broadcast_to(row, (n, n)), 0.0), axis=1, keepdims=True)


def swap_bits(x, row_step, lane_step):
    rows, lanes = x.shape
    row_bit = (iota(x.shape, 0) // row_step) % 2
    lane_bit = (iota(x.shape, 1) // lane_step) % 2
    down = pltpu.roll(pltpu.roll(x, rows - row_step, 0), lane_step, 1)
    up = pltpu.roll(pltpu.roll(x, row_step, 0), lanes - lane_step, 1)
    return jnp.where(row_bit == lane_bit, x, jnp.where(row_bit == 0, down, up))


def lane_shift(x, step):
    edge = iota((x.shape[0], LANES), 1) == (0 if step == 1 else LANES - 1)
    moved = [
        jnp.where(edge, jnp.zeros_like(part), pltpu.roll(part, step % LANES, 1))
        for part in (x[:, i : i + LANES] for i in range(0, x.shape[1], LANES))
    ]
    return jnp.concatenate(moved, axis=1)


def input_layer(rows, order, weights, put):
    rows = jnp.concatenate([rows[w].astype(F32) for w in range(WIN)], axis=0).astype(BF16)
    rows = jnp.dot(rows, order, preferred_element_type=F32)
    lines = [
        jnp.concatenate(
            [rows[OWN * w : OWN * (w + 1), v * LANES : (v + 1) * LANES] for w in range(WIN)], axis=1
        )
        for v in range(PH)
    ]
    for v in range(PH):
        before = lines[v - 1] if v > 0 else lane_shift(lines[PH - 1], 1)
        after = lines[v + 1] if v < PH - 1 else lane_shift(lines[0], -1)
        taps = jnp.concatenate([before, lines[v], after], axis=0).astype(BF16)
        put(v, jnp.dot(weights, taps, preferred_element_type=F32).astype(BF16))


def prepare_kernel(
    cut_ref, conv_any, in_any, out_any, sources_any, raw_any, order_any, flags_any, perm_any,
    band_ref, first_ref, last_ref, one_hot_ref, raw_ref, order_ref, flags_ref, perm_ref,
    conv_ref, in_ref, out_ref, sources_ref, sems,
):
    pairs = (
        (conv_any, conv_ref), (in_any, in_ref), (out_any, out_ref), (sources_any, sources_ref),
        (raw_any, raw_ref), (order_any, order_ref), (flags_any, flags_ref), (perm_any, perm_ref),
    )
    copies = [pltpu.make_async_copy(a, b, sems.at[i]) for i, (a, b) in enumerate(pairs)]
    for copy in copies:
        copy.start()
    copies[1].wait()
    half = EXT // 2
    shape = (half * F, 3 * OWN)
    channel, lane = iota(shape, 0) // F, iota(shape, 1)
    talls = []
    for tap in range(3):
        weight = column(in_ref[tap : tap + 1, :].astype(F32), F)
        talls.append(jnp.broadcast_to(jnp.concatenate([weight] * half, axis=0), shape))
    for i, place in enumerate((channel + 1, channel)):
        first = jnp.zeros(shape, F32)
        for tap in range(3):
            first = jnp.where(lane == place + OWN * tap, talls[tap], first)
        first_ref[i] = first.astype(BF16)
    copies[2].wait()
    shape = (OWN, OWN * F)
    wide = jnp.concatenate([out_ref[...].astype(F32)] * OWN, axis=1)
    last_ref[...] = jnp.where(
        iota(shape, 0) == iota(shape, 1) // F, jnp.broadcast_to(wide, shape), 0.0
    ).astype(BF16)
    copies[3].wait()
    shape = (CH_ALL, NV)
    j = (sources_ref[...] + OWN // 2) % CH_ALL
    z = ((j // 16) % 16 - Z_ORDER[0]) % 16
    row = (j // 256) * 256 + ((j // 8) % 2) * 128 + (j % 8) * 16 + z
    one_hot_ref[...] = jnp.where(iota(shape, 0) == jnp.broadcast_to(row, shape), 1.0, 0.0).astype(BF16)
    copies[0].wait()
    for layer in range(LAYERS):
        for tap in range(3):
            taps = [conv_ref[layer, a, tap] for a in range(3)]
            base = jnp.concatenate(taps + [jnp.zeros((F, 256 - 3 * F), BF16)], axis=1)
            for c in range(BLK):
                row = base if c == 0 else pltpu.roll(base, F * c, 1)
                for block in range(2):
                    band_ref[layer, block, F * c : F * (c + 1), 256 * tap : 256 * (tap + 1)] = row

    @pl.when(cut_ref[0] == 1)
    def _():
        for layer in range(LAYERS):
            for block in range(2):
                start = block * (EXT - 2 * (layer + 1) - BLK) + layer
                for c, k in ((5 - start, 7 - start), (6 - start, 6 - start)):
                    if 0 <= c < BLK:
                        for tap in range(3):
                            lanes = slice(256 * tap + F * k, 256 * tap + F * (k + 1))
                            band_ref[layer, block, F * c : F * (c + 1), lanes] = jnp.zeros((F, F), BF16)

    for copy in copies[4:]:
        copy.wait()


def denoise_kernel(
    before_ref, before_flags_ref, raw_ref, flags_ref, order_ref, band_ref, first_ref, last_ref, table_any,
    out_ref, h0_ref, h1_ref, h2_ref, h3_ref, earlier_ref, later_ref, line_ref, table_ref, sem,
):
    table_copy = pltpu.make_async_copy(table_any, table_ref, sem)
    table_copy.start()
    hidden = (h0_ref, h1_ref, h2_ref, h3_ref)
    chunk = [slice(v * CHUNK, (v + 1) * CHUNK) for v in range(PH)]
    for i, ref in enumerate((before_ref, raw_ref)):
        rows = slice(i * EXT // 2 * F, (i + 1) * EXT // 2 * F)

        def put(v, value, rows=rows):
            h0_ref[rows, chunk[v]] = value

        input_layer(ref, order_ref[...], first_ref[i], put)
    for layer in range(LAYERS):
        step = 2**layer
        source, target = hidden[layer], hidden[layer + 1]
        size = (EXT - 2 * layer) * F
        count = EXT - 2 * (layer + 1)
        for v in sorted(range(PH), key=lambda v: (v < step) + (v >= PH - step)):
            before, after, u, t = source, source, v - step, v + step
            if u < 0:
                u += PH
                before = earlier_ref
                earlier_ref[:size, chunk[u]] = lane_shift(source[:, chunk[u]], 1)
            if t >= PH:
                t -= PH
                after = later_ref
                later_ref[:size, chunk[t]] = lane_shift(source[:, chunk[t]], -1)
            for block, start, low in ((0, 0, 0), (1, count - BLK, 2 * BLK - count)):
                k = slice(start * F, (start + BLK + 2) * F)
                taps = jnp.concatenate([before[k, chunk[u]], source[k, chunk[v]], after[k, chunk[t]]], axis=0)
                total = jnp.dot(band_ref[layer, block, low * F :, :], taps, preferred_element_type=F32)
                old = source[(start + low + 1) * F : (start + BLK + 1) * F, chunk[v]].astype(F32)
                new = old + jnp.maximum(total, 0.0)
                for i in range(BLK - low):
                    c = start + low + i
                    target[c * F : (c + 1) * F, chunk[v]] = new[i * F : (i + 1) * F].astype(BF16)
    clean = jnp.dot(last_ref[...], h3_ref[...], preferred_element_type=F32)
    clean = jnp.concatenate(
        [
            jnp.concatenate(
                [clean[:, v * CHUNK + w * LANES : v * CHUNK + (w + 1) * LANES] for v in range(PH)], axis=1
            )
            for w in range(WIN)
        ],
        axis=0,
    )
    table_copy.wait()
    spectra = jnp.dot(clean.astype(BF16), table_ref[...], preferred_element_type=F32)
    real, imag = spectra[:, :NF], spectra[:, NF:]
    power = real * real + imag * imag
    spread = jnp.sqrt(jnp.mean(power, axis=1, keepdims=True) + epsilon_power)
    flags = jnp.concatenate(
        [
            column(ref[w : w + 1, :].astype(F32), OWN)[part]
            for w in range(WIN)
            for ref, part in ((before_flags_ref, slice(4, 8)), (flags_ref, slice(0, 4)))
        ],
        axis=0,
    )
    factor = flags / (jnp.sqrt(power) + water_level * spread)
    for part, value in enumerate((real * factor, imag * factor)):
        for w in range(WIN):
            for high in range(2):
                x = value[w * OWN : (w + 1) * OWN, high * 128 : (high + 1) * 128]
                for bit in range(3):
                    x = swap_bits(x, 2**bit, 16 * 2**bit)
                line_ref[pl.ds(32 * high + 2 * w + part, 8, stride=4), :] = x
    out_ref[...] = line_ref[...].astype(BF16)


def turn_kernel(in_ref, out_ref):
    x = in_ref[...].astype(F32)
    for bit in range(4):
        x = swap_bits(x, 4 * 2**bit, 2**bit)
    x = x.astype(BF16)
    out_ref[:64, :] = x
    out_ref[64:, :] = x


def coherence_kernel(half_ref, one_hot_ref, perm_ref, in_ref, out_any, all_ref, out_ref, sems):
    x = in_ref[...].astype(F32)

    def piece(w, c, y):
        start = ((w * 2 + c) * 4 + Y_ORDER.index(y)) * 8
        return x[start : start + 8]

    stacked = jnp.concatenate(
        [
            jnp.concatenate([piece(w, c, y) for y in range(4) for w in range(2)], axis=0)
            for c in range(2)
        ],
        axis=1,
    ).astype(BF16)
    ordered = jnp.dot(stacked, perm_ref[...], preferred_element_type=F32)
    every = jnp.concatenate([ordered[16 * y : 16 * (y + 1)] for y in range(4)], axis=1)
    all_ref[...] = pltpu.roll(every, CH_ALL - OWN // 2, 1)
    half = half_ref[0]
    receivers = all_ref[:, pl.ds(pl.multiple_of(half * 512, 512), 512)]
    gathered = jnp.concatenate([stacked[16 * y : 16 * (y + 1)] for y in range(4)], axis=1)
    chosen = jnp.dot(gathered, one_hot_ref[...], preferred_element_type=F32)
    even = iota(receivers.shape, 0) % 2 == 0
    turned = jnp.where(even, pltpu.roll(receivers, 15, 0), -pltpu.roll(receivers, 1, 0))
    chosen_t = chosen.T
    energy_src = jnp.sum(chosen_t * chosen_t, axis=1, keepdims=True)
    energy_rec = jnp.sum(receivers * receivers, axis=0, keepdims=True)
    scale = lax.rsqrt(jnp.maximum(energy_src * energy_rec, 1.0))
    left = chosen_t.astype(BF16)
    copies = []
    for part, right in enumerate((receivers, turned)):
        out_ref[part] = jnp.dot(left, right.astype(BF16), preferred_element_type=F32) * scale
        copies.append(pltpu.make_async_copy(out_ref.at[part], out_any.at[0, part], sems.at[part]))
        copies[-1].start()
    for copy in copies:
        copy.wait()


VMEM = pl.BlockSpec(memory_space=pltpu.VMEM)
SMEM = pl.BlockSpec(memory_space=pltpu.SMEM)
PARAMS = pltpu.CompilerParams(vmem_limit_bytes=16 * 1024 * 1024)


def prepare(cut, conv_weight, in_weight, out_weight, sources, raw, flags):
    arrays = (
        conv_weight.transpose(0, 3, 4, 1, 2), in_weight.T, out_weight.reshape(1, F), sources.reshape(1, NV),
        raw, jnp.asarray(sample_perm()), flags, jnp.asarray(channel_perm()),
    )
    arrays = tuple(pltpu.with_memory_space_constraint(a, pltpu.HBM) for a in arrays)
    return pl.pallas_call(
        prepare_kernel,
        out_shape=(
            jax.ShapeDtypeStruct((LAYERS, 2, BLK * F, 3 * 256), BF16),
            jax.ShapeDtypeStruct((2, EXT // 2 * F, 3 * OWN), BF16),
            jax.ShapeDtypeStruct((OWN, OWN * F), BF16),
            jax.ShapeDtypeStruct((CH_ALL, NV), BF16),
        )
        + tuple(jax.ShapeDtypeStruct(a.shape, a.dtype) for a in arrays[4:]),
        in_specs=[SMEM] + [pl.BlockSpec(memory_space=pl.ANY)] * 8,
        out_specs=(VMEM,) * 8,
        scratch_shapes=[pltpu.VMEM(a.shape, a.dtype) for a in arrays[:4]]
        + [pltpu.SemaphoreType.DMA((8,))],
        compiler_params=PARAMS,
        cost_estimate=pl.CostEstimate(flops=2_000_000, bytes_accessed=4_000_000, transcendentals=0),
        name="prepare",
    )(cut, *arrays)


def denoise(before, before_flags, raw, flags, order, band, first, last):
    table = pltpu.with_memory_space_constraint(jnp.asarray(dft_table()), pltpu.HBM)
    return pl.pallas_call(
        denoise_kernel,
        out_shape=jax.ShapeDtypeStruct((64, 128), BF16),
        in_specs=[VMEM] * 8 + [pl.BlockSpec(memory_space=pl.ANY)],
        out_specs=VMEM,
        scratch_shapes=[pltpu.VMEM(((EXT - 2 * i) * F, WIDE), BF16) for i in range(LAYERS + 1)]
        + [pltpu.VMEM((EXT * F, WIDE), BF16)] * 2
        + [pltpu.VMEM((64, 128), F32), pltpu.VMEM(table.shape, BF16), pltpu.SemaphoreType.DMA],
        compiler_params=PARAMS,
        name="denoise",
    )(before, before_flags, raw, flags, order, band, first, last, table)


def turn(rows):
    return pl.pallas_call(
        turn_kernel,
        out_shape=jax.ShapeDtypeStruct((128, 128), BF16),
        in_specs=[VMEM],
        out_specs=VMEM,
        compiler_params=PARAMS,
        name="turn",
    )(rows)


def coherence(half, one_hot, perm, rows):
    return pl.pallas_call(
        coherence_kernel,
        out_shape=jax.ShapeDtypeStruct((1, 2, 128, 512), F32),
        in_specs=[SMEM, VMEM, VMEM, VMEM],
        out_specs=pl.BlockSpec(memory_space=pl.ANY),
        scratch_shapes=[
            pltpu.VMEM((16, CH_ALL), F32),
            pltpu.VMEM((2, 128, 512), F32),
            pltpu.SemaphoreType.DMA((2,)),
        ],
        compiler_params=PARAMS,
        name="coherence",
    )(half, one_hot, perm, rows)


CHAN = ("y", "z", "c")


def per_device(raw, flags, in_weight, conv_weight, out_weight, sources):
    count = lax.axis_size(CHAN)
    ring = [(i, (i + 1) % count) for i in range(count)]
    before = lax.ppermute(raw, CHAN, ring)
    before_flags = lax.ppermute(flags, CHAN, ring)
    cut = (lax.axis_index(CHAN) == 0).astype(jnp.int32).reshape(1)
    half = lax.axis_index("w").reshape(1).astype(jnp.int32)
    band, first, last, one_hot, raw, order, flags, perm = prepare(
        cut, conv_weight, in_weight, out_weight, sources, raw, flags
    )
    sent = denoise(before, before_flags, raw, flags, order, band, first, last)
    half, sent = lax.optimization_barrier((half, sent))
    got = lax.all_to_all(
        sent, "z", 0, 0, tiled=True, axis_index_groups=[[int(z) for z in Z_ORDER]]
    )
    rest = [((w * 2 + c) * 4 + y) * 2 + s for w in W_ORDER for c in range(2) for y in Y_ORDER for s in range(2)]
    mine = lax.all_to_all(turn(got), ("w", "c", "y", "s"), 0, 0, tiled=True, axis_index_groups=[rest])
    return coherence(half, one_hot, perm, mine)


def solution(mesh):
    fine = Mesh(mesh.devices.reshape(2, 4, 16, 2, 2), ("s", "y", "z", "c", "w"))
    placed = (P(("s", "w"), CHAN, None), P(("s", "w"), CHAN), P(), P(), P(), P())
    return jax.shard_map(
        per_device,
        mesh=fine,
        in_specs=placed,
        out_specs=P(("s",) + CHAN, None, None, "w"),
        check_vma=False,
    )
```

```python
import functools
import math

import jax
import jax.numpy as jnp
import numpy as np
from jax import lax
from jax.experimental import pallas as pl
from jax.experimental.pallas import tpu as pltpu
from jax.sharding import Mesh, PartitionSpec as P

NT = 640
F = 32
LAYERS = 3
NF = 256
OWN = 8
WIN = 2
EXT = OWN + 2 * LAYERS
BLK = 6
LANES = 128
PH = NT // LANES
CHUNK = WIN * LANES
WIDE = WIN * NT
CH_ALL = 1024
NV = 128
Y_ORDER = (2, 3, 0, 1)
W_ORDER = (1, 0)
Z_ORDER = tuple((np.arange(16) + 8) % 16)

water_level = 0.2
epsilon_power = 1e-06

F32 = jnp.float32
BF16 = jnp.bfloat16


def dft_table():
    part, z, core, y, section = np.meshgrid(
        np.arange(2), np.array(Z_ORDER), np.arange(2), np.array(Y_ORDER), np.arange(2), indexing="ij"
    )
    k = (section * 128 + (y * 16 + z) * 2 + core).reshape(-1)
    part = part.reshape(-1)
    phases = np.arange(NT)[:, None] * (k + 1)[None, :] % NT
    angles = phases.astype(np.float32) * np.float32(2.0 * math.pi / NT)
    table = np.where(part[None, :] == 0, np.cos(angles), -np.sin(angles))
    return table[sample_order()].astype(BF16)


def sample_order():
    return (np.arange(LANES)[None, :] * PH + np.arange(PH)[:, None]).reshape(-1)


def sample_perm():
    return np.eye(NT, dtype=np.float32)[:, sample_order()].astype(BF16)


def channel_perm():
    core, channel, z = np.meshgrid(np.arange(2), np.arange(OWN), np.array(Z_ORDER), indexing="ij")
    target = ((z * 2 + core) * OWN + channel).reshape(-1)
    return np.eye(256, dtype=np.float32)[target].astype(BF16)


def iota(shape, dim):
    return lax.broadcasted_iota(jnp.int32, shape, dim)


def column(row, n):
    eye = iota((n, n), 0) == iota((n, n), 1)
    return jnp.sum(jnp.where(eye, jnp.broadcast_to(row, (n, n)), 0.0), axis=1, keepdims=True)


def swap_bits(x, row_step, lane_step):
    rows, lanes = x.shape
    row_bit = (iota(x.shape, 0) // row_step) % 2
    lane_bit = (iota(x.shape, 1) // lane_step) % 2
    down = pltpu.roll(pltpu.roll(x, rows - row_step, 0), lane_step, 1)
    up = pltpu.roll(pltpu.roll(x, row_step, 0), lanes - lane_step, 1)
    return jnp.where(row_bit == lane_bit, x, jnp.where(row_bit == 0, down, up))


def pack_kernel(raw_any, flags_any, own_ref, flags_ref, sems):
    copies = (
        pltpu.make_async_copy(flags_any, flags_ref, sems.at[0]),
        pltpu.make_async_copy(raw_any, own_ref.at[:, :, pl.ds(0, NT)], sems.at[1]),
    )
    for copy in copies:
        copy.start()
    copies[0].wait()
    for w in range(WIN):
        flags = column(flags_ref[w : w + 1, :].astype(F32), OWN)
        own_ref[w, :, NT:] = jnp.broadcast_to(flags, (OWN, LANES)).astype(BF16)
    copies[1].wait()


def prepare_kernel(
    cut_ref, conv_any, in_any, out_any, sources_any, order_any, table_any, perm_any,
    band_ref, first_ref, last_ref, one_hot_ref, order_ref, table_ref, perm_ref,
    conv_ref, in_ref, out_ref, sources_ref, sems,
):
    pairs = (
        (conv_any, conv_ref), (in_any, in_ref), (out_any, out_ref), (sources_any, sources_ref),
        (order_any, order_ref), (table_any, table_ref), (perm_any, perm_ref),
    )
    copies = [pltpu.make_async_copy(a, b, sems.at[i]) for i, (a, b) in enumerate(pairs)]
    for copy in copies:
        copy.start()
    copies[1].wait()
    shape = (EXT * F, 48)
    channel = iota(shape, 0) // F
    place = jnp.where(channel < 7, OWN + 1 + channel, channel - 7)
    lane = iota(shape, 1)
    first = jnp.zeros(shape, F32)
    for tap in range(3):
        weight = column(in_ref[tap : tap + 1, :].astype(F32), F)
        tall = jnp.broadcast_to(jnp.concatenate([weight] * EXT, axis=0), shape)
        first = jnp.where(lane == place + 16 * tap, tall, first)
    first_ref[...] = first.astype(BF16)
    copies[2].wait()
    shape = (OWN, OWN * F)
    wide = jnp.concatenate([out_ref[...].astype(F32)] * OWN, axis=1)
    last_ref[...] = jnp.where(
        iota(shape, 0) == iota(shape, 1) // F, jnp.broadcast_to(wide, shape), 0.0
    ).astype(BF16)
    copies[3].wait()
    shape = (CH_ALL, NV)
    j = (sources_ref[...] + OWN // 2) % CH_ALL
    z = ((j // 16) % 16 - Z_ORDER[0]) % 16
    row = (j // 256) * 256 + ((j // 8) % 2) * 128 + (j % 8) * 16 + z
    one_hot_ref[...] = jnp.where(iota(shape, 0) == jnp.broadcast_to(row, shape), 1.0, 0.0).astype(BF16)
    copies[0].wait()
    for layer in range(LAYERS):
        for tap in range(3):
            taps = [conv_ref[layer, a, tap] for a in range(3)]
            base = jnp.concatenate(taps + [jnp.zeros((F, 256 - 3 * F), BF16)], axis=1)
            for c in range(BLK):
                row = base if c == 0 else pltpu.roll(base, F * c, 1)
                for block in range(2):
                    band_ref[layer, block, F * c : F * (c + 1), 256 * tap : 256 * (tap + 1)] = row

    @pl.when(cut_ref[0] == 1)
    def _():
        for layer in range(LAYERS):
            for block in range(2):
                start = block * (EXT - 2 * (layer + 1) - BLK) + layer
                for c, k in ((5 - start, 7 - start), (6 - start, 6 - start)):
                    if 0 <= c < BLK:
                        for tap in range(3):
                            lanes = slice(256 * tap + F * k, 256 * tap + F * (k + 1))
                            band_ref[layer, block, F * c : F * (c + 1), lanes] = jnp.zeros((F, F), BF16)

    for copy in copies[4:]:
        copy.wait()


def lane_shift(x, step):
    edge = iota((x.shape[0], LANES), 1) == (0 if step == 1 else LANES - 1)
    moved = [
        jnp.where(edge, jnp.zeros_like(part), pltpu.roll(part, step % LANES, 1))
        for part in (x[:, i : i + LANES] for i in range(0, x.shape[1], LANES))
    ]
    return jnp.concatenate(moved, axis=1)


def denoise_kernel(
    own_ref, left_ref, order_ref, band_ref, first_ref, last_ref, table_ref,
    out_ref, h0_ref, h1_ref, h2_ref, h3_ref, earlier_ref, later_ref, line_ref,
):
    rows = [ref[w, :, :NT].astype(F32) for w in range(WIN) for ref in (own_ref, left_ref)]
    rows = jnp.concatenate(rows, axis=0).astype(BF16)
    rows = jnp.dot(rows, order_ref[...], preferred_element_type=F32)
    lines = [
        jnp.concatenate(
            [rows[16 * w : 16 * (w + 1), v * LANES : (v + 1) * LANES] for w in range(WIN)], axis=1
        )
        for v in range(PH)
    ]
    hidden = (h0_ref, h1_ref, h2_ref, h3_ref)
    chunk = [slice(v * CHUNK, (v + 1) * CHUNK) for v in range(PH)]
    for v in range(PH):
        before = lines[v - 1] if v > 0 else lane_shift(lines[PH - 1], 1)
        after = lines[v + 1] if v < PH - 1 else lane_shift(lines[0], -1)
        taps = jnp.concatenate([before, lines[v], after], axis=0).astype(BF16)
        h0_ref[:, chunk[v]] = jnp.dot(first_ref[...], taps, preferred_element_type=F32).astype(BF16)
    for layer in range(LAYERS):
        step = 2**layer
        source, target = hidden[layer], hidden[layer + 1]
        size = (EXT - 2 * layer) * F
        count = EXT - 2 * (layer + 1)
        for v in sorted(range(PH), key=lambda v: (v < step) + (v >= PH - step)):
            before, after, u, t = source, source, v - step, v + step
            if u < 0:
                u += PH
                before = earlier_ref
                earlier_ref[:size, chunk[u]] = lane_shift(source[:, chunk[u]], 1)
            if t >= PH:
                t -= PH
                after = later_ref
                later_ref[:size, chunk[t]] = lane_shift(source[:, chunk[t]], -1)
            for block, start, low in ((0, 0, 0), (1, count - BLK, 2 * BLK - count)):
                k = slice(start * F, (start + BLK + 2) * F)
                taps = jnp.concatenate([before[k, chunk[u]], source[k, chunk[v]], after[k, chunk[t]]], axis=0)
                total = jnp.dot(band_ref[layer, block, low * F :, :], taps, preferred_element_type=F32)
                old = source[(start + low + 1) * F : (start + BLK + 1) * F, chunk[v]].astype(F32)
                new = old + jnp.maximum(total, 0.0)
                for i in range(BLK - low):
                    c = start + low + i
                    target[c * F : (c + 1) * F, chunk[v]] = new[i * F : (i + 1) * F].astype(BF16)
    clean = jnp.dot(last_ref[...], h3_ref[...], preferred_element_type=F32)
    clean = jnp.concatenate(
        [
            jnp.concatenate(
                [clean[:, v * CHUNK + w * LANES : v * CHUNK + (w + 1) * LANES] for v in range(PH)], axis=1
            )
            for w in range(WIN)
        ],
        axis=0,
    )
    spectra = jnp.dot(clean.astype(BF16), table_ref[...], preferred_element_type=F32)
    real, imag = spectra[:, :NF], spectra[:, NF:]
    power = real * real + imag * imag
    spread = jnp.sqrt(jnp.mean(power, axis=1, keepdims=True) + epsilon_power)
    flags = jnp.concatenate(
        [
            ref[w, :, NT : NT + 1].astype(F32)[part]
            for w in range(WIN)
            for ref, part in ((left_ref, slice(4, 8)), (own_ref, slice(0, 4)))
        ],
        axis=0,
    )
    factor = flags / (jnp.sqrt(power) + water_level * spread)
    for part, value in enumerate((real * factor, imag * factor)):
        for w in range(WIN):
            for high in range(2):
                x = value[w * OWN : (w + 1) * OWN, high * 128 : (high + 1) * 128]
                for bit in range(3):
                    x = swap_bits(x, 2**bit, 16 * 2**bit)
                line_ref[pl.ds(32 * high + 2 * w + part, 8, stride=4), :] = x
    out_ref[...] = line_ref[...].astype(BF16)


def turn_kernel(in_ref, out_ref):
    x = in_ref[...].astype(F32)
    for bit in range(4):
        x = swap_bits(x, 4 * 2**bit, 2**bit)
    x = x.astype(BF16)
    out_ref[:64, :] = x
    out_ref[64:, :] = x


def coherence_kernel(half_ref, one_hot_ref, perm_ref, in_ref, out_any, all_ref, out_ref, sems):
    x = in_ref[...].astype(F32)

    def piece(w, c, y):
        start = ((w * 2 + c) * 4 + Y_ORDER.index(y)) * 8
        return x[start : start + 8]

    stacked = jnp.concatenate(
        [
            jnp.concatenate([piece(w, c, y) for y in range(4) for w in range(2)], axis=0)
            for c in range(2)
        ],
        axis=1,
    ).astype(BF16)
    ordered = jnp.dot(stacked, perm_ref[...], preferred_element_type=F32)
    every = jnp.concatenate([ordered[16 * y : 16 * (y + 1)] for y in range(4)], axis=1)
    all_ref[...] = pltpu.roll(every, CH_ALL - OWN // 2, 1)
    half = half_ref[0]
    receivers = all_ref[:, pl.ds(pl.multiple_of(half * 512, 512), 512)]
    gathered = jnp.concatenate([stacked[16 * y : 16 * (y + 1)] for y in range(4)], axis=1)
    chosen = jnp.dot(gathered, one_hot_ref[...], preferred_element_type=F32)
    even = iota(receivers.shape, 0) % 2 == 0
    turned = jnp.where(even, pltpu.roll(receivers, 15, 0), -pltpu.roll(receivers, 1, 0))
    chosen_t = chosen.T
    energy_src = jnp.sum(chosen_t * chosen_t, axis=1, keepdims=True)
    energy_rec = jnp.sum(receivers * receivers, axis=0, keepdims=True)
    scale = lax.rsqrt(jnp.maximum(energy_src * energy_rec, 1.0))
    left = chosen_t.astype(BF16)
    copies = []
    for part, right in enumerate((receivers, turned)):
        out_ref[part] = jnp.dot(left, right.astype(BF16), preferred_element_type=F32) * scale
        copies.append(pltpu.make_async_copy(out_ref.at[part], out_any.at[0, part], sems.at[part]))
        copies[-1].start()
    for copy in copies:
        copy.wait()


VMEM = pl.BlockSpec(memory_space=pltpu.VMEM)
SMEM = pl.BlockSpec(memory_space=pltpu.SMEM)
PARAMS = pltpu.CompilerParams(vmem_limit_bytes=32 * 1024 * 1024)


def pack(raw, flags):
    raw, flags = (pltpu.with_memory_space_constraint(a, pltpu.HBM) for a in (raw, flags))
    return pl.pallas_call(
        pack_kernel,
        out_shape=jax.ShapeDtypeStruct((WIN, OWN, NT + LANES), BF16),
        in_specs=[pl.BlockSpec(memory_space=pl.ANY)] * 2,
        out_specs=VMEM,
        scratch_shapes=[pltpu.VMEM(flags.shape, flags.dtype), pltpu.SemaphoreType.DMA((2,))],
        compiler_params=PARAMS,
        name="pack",
    )(raw, flags)


def prepare(cut, conv_weight, in_weight, out_weight, sources):
    arrays = (
        conv_weight.transpose(0, 3, 4, 1, 2), in_weight.T, out_weight.reshape(1, F), sources.reshape(1, NV),
        jnp.asarray(sample_perm()), jnp.asarray(dft_table()), jnp.asarray(channel_perm()),
    )
    arrays = tuple(pltpu.with_memory_space_constraint(a, pltpu.HBM) for a in arrays)
    return pl.pallas_call(
        prepare_kernel,
        out_shape=(
            jax.ShapeDtypeStruct((LAYERS, 2, BLK * F, 3 * 256), BF16),
            jax.ShapeDtypeStruct((EXT * F, 48), BF16),
            jax.ShapeDtypeStruct((OWN, OWN * F), BF16),
            jax.ShapeDtypeStruct((CH_ALL, NV), BF16),
        )
        + tuple(jax.ShapeDtypeStruct(a.shape, a.dtype) for a in arrays[4:]),
        in_specs=[SMEM] + [pl.BlockSpec(memory_space=pl.ANY)] * 7,
        out_specs=(VMEM,) * 7,
        scratch_shapes=[pltpu.VMEM(a.shape, a.dtype) for a in arrays[:4]]
        + [pltpu.SemaphoreType.DMA((7,))],
        compiler_params=PARAMS,
        cost_estimate=pl.CostEstimate(flops=2_000_000, bytes_accessed=4_000_000, transcendentals=0),
        name="prepare",
    )(cut, *arrays)


def denoise(own, left, order, band, first, last, table):
    return pl.pallas_call(
        denoise_kernel,
        out_shape=jax.ShapeDtypeStruct((64, 128), BF16),
        in_specs=[VMEM] * 7,
        out_specs=VMEM,
        scratch_shapes=[pltpu.VMEM(((EXT - 2 * i) * F, WIDE), BF16) for i in range(LAYERS + 1)]
        + [pltpu.VMEM((EXT * F, WIDE), BF16)] * 2
        + [pltpu.VMEM((64, 128), F32)],
        compiler_params=PARAMS,
        name="denoise",
    )(own, left, order, band, first, last, table)


def turn(rows):
    return pl.pallas_call(
        turn_kernel,
        out_shape=jax.ShapeDtypeStruct((128, 128), BF16),
        in_specs=[VMEM],
        out_specs=VMEM,
        compiler_params=PARAMS,
        name="turn",
    )(rows)


def coherence(half, one_hot, perm, rows):
    return pl.pallas_call(
        coherence_kernel,
        out_shape=jax.ShapeDtypeStruct((1, 2, 128, 512), F32),
        in_specs=[SMEM, VMEM, VMEM, VMEM],
        out_specs=pl.BlockSpec(memory_space=pl.ANY),
        scratch_shapes=[
            pltpu.VMEM((16, CH_ALL), F32),
            pltpu.VMEM((2, 128, 512), F32),
            pltpu.SemaphoreType.DMA((2,)),
        ],
        compiler_params=PARAMS,
        name="coherence",
    )(half, one_hot, perm, rows)


CHAN = ("y", "z", "c")


def per_device(raw, flags, in_weight, conv_weight, out_weight, sources):
    count = lax.axis_size(CHAN)
    own = pack(raw, flags)
    left = lax.ppermute(own, CHAN, [(i, (i + 1) % count) for i in range(count)])
    cut = (lax.axis_index(CHAN) == 0).astype(jnp.int32).reshape(1)
    half = lax.axis_index("w").reshape(1).astype(jnp.int32)
    band, first, last, one_hot, order, table, perm = prepare(cut, conv_weight, in_weight, out_weight, sources)
    sent = denoise(own, left, order, band, first, last, table)
    half, sent = lax.optimization_barrier((half, sent))
    got = lax.all_to_all(
        sent, "z", 0, 0, tiled=True, axis_index_groups=[[int(z) for z in Z_ORDER]]
    )
    rest = [((w * 2 + c) * 4 + y) * 2 + s for w in W_ORDER for c in range(2) for y in Y_ORDER for s in range(2)]
    mine = lax.all_to_all(turn(got), ("w", "c", "y", "s"), 0, 0, tiled=True, axis_index_groups=[rest])
    return coherence(half, one_hot, perm, mine)


def solution(mesh):
    fine = Mesh(mesh.devices.reshape(2, 4, 16, 2, 2), ("s", "y", "z", "c", "w"))
    placed = (P(("s", "w"), CHAN, None), P(("s", "w"), CHAN), P(), P(), P(), P())
    return jax.shard_map(
        per_device,
        mesh=fine,
        in_specs=placed,
        out_specs=P(("s",) + CHAN, None, None, "w"),
        check_vma=False,
    )
```

```python
import functools
import math

import jax
import jax.numpy as jnp
import numpy as np
from jax import lax
from jax.experimental import pallas as pl
from jax.experimental.pallas import tpu as pltpu
from jax.sharding import Mesh, PartitionSpec as P

NT = 640
F = 32
LAYERS = 3
NF = 256
OWN = 8
WIN = 2
EXT = OWN + 2 * LAYERS
BLK = 6
LANES = 128
PH = NT // LANES
CHUNK = WIN * LANES
WIDE = WIN * NT
CH_ALL = 1024
NV = 128
Y_ORDER = (2, 3, 0, 1)
W_ORDER = (1, 0)
Z_ORDER = (8, 0, 1, 15, 2, 14, 3, 13, 4, 12, 5, 11, 6, 10, 7, 9)

water_level = 0.2
epsilon_power = 1e-06

F32 = jnp.float32
BF16 = jnp.bfloat16


def dft_table():
    part, z, core, y, section = np.meshgrid(
        np.arange(2), np.array(Z_ORDER), np.arange(2), np.array(Y_ORDER), np.arange(2), indexing="ij"
    )
    k = (section * 128 + (y * 16 + z) * 2 + core).reshape(-1)
    part = part.reshape(-1)
    phases = np.arange(NT)[:, None] * (k + 1)[None, :] % NT
    angles = phases.astype(np.float32) * np.float32(2.0 * math.pi / NT)
    table = np.where(part[None, :] == 0, np.cos(angles), -np.sin(angles))
    return table[sample_order()].astype(BF16)


def sample_order():
    return (np.arange(LANES)[None, :] * PH + np.arange(PH)[:, None]).reshape(-1)


def sample_perm():
    return np.eye(NT, dtype=np.float32)[:, sample_order()].astype(BF16)


def channel_perm():
    core, channel, z = np.meshgrid(np.arange(2), np.arange(OWN), np.array(Z_ORDER), indexing="ij")
    target = ((z * 2 + core) * OWN + channel).reshape(-1)
    return np.eye(256, dtype=np.float32)[target].astype(BF16)


def iota(shape, dim):
    return lax.broadcasted_iota(jnp.int32, shape, dim)


def column(row, n):
    eye = iota((n, n), 0) == iota((n, n), 1)
    return jnp.sum(jnp.where(eye, jnp.broadcast_to(row, (n, n)), 0.0), axis=1, keepdims=True)


def swap_bits(x, row_step, lane_step):
    rows, lanes = x.shape
    row_bit = (iota(x.shape, 0) // row_step) % 2
    lane_bit = (iota(x.shape, 1) // lane_step) % 2
    down = pltpu.roll(pltpu.roll(x, rows - row_step, 0), lane_step, 1)
    up = pltpu.roll(pltpu.roll(x, row_step, 0), lanes - lane_step, 1)
    return jnp.where(row_bit == lane_bit, x, jnp.where(row_bit == 0, down, up))


def pack_kernel(raw_any, flags_any, own_ref, flags_ref, sems):
    copies = (
        pltpu.make_async_copy(flags_any, flags_ref, sems.at[0]),
        pltpu.make_async_copy(raw_any, own_ref.at[:, :, pl.ds(0, NT)], sems.at[1]),
    )
    for copy in copies:
        copy.start()
    copies[0].wait()
    for w in range(WIN):
        flags = column(flags_ref[w : w + 1, :].astype(F32), OWN)
        own_ref[w, :, NT:] = jnp.broadcast_to(flags, (OWN, LANES)).astype(BF16)
    copies[1].wait()


def prepare_kernel(
    cut_ref, conv_any, in_any, out_any, sources_any, order_any, table_any, perm_any,
    band_ref, first_ref, last_ref, one_hot_ref, order_ref, table_ref, perm_ref,
    conv_ref, in_ref, out_ref, sources_ref, sems,
):
    pairs = (
        (conv_any, conv_ref), (in_any, in_ref), (out_any, out_ref), (sources_any, sources_ref),
        (order_any, order_ref), (table_any, table_ref), (perm_any, perm_ref),
    )
    copies = [pltpu.make_async_copy(a, b, sems.at[i]) for i, (a, b) in enumerate(pairs)]
    for copy in copies:
        copy.start()
    copies[1].wait()
    shape = (EXT * F, 48)
    channel = iota(shape, 0) // F
    place = jnp.where(channel < 7, OWN + 1 + channel, channel - 7)
    lane = iota(shape, 1)
    first = jnp.zeros(shape, F32)
    for tap in range(3):
        weight = column(in_ref[tap : tap + 1, :].astype(F32), F)
        tall = jnp.broadcast_to(jnp.concatenate([weight] * EXT, axis=0), shape)
        first = jnp.where(lane == place + 16 * tap, tall, first)
    first_ref[...] = first.astype(BF16)
    copies[2].wait()
    shape = (OWN, OWN * F)
    wide = jnp.concatenate([out_ref[...].astype(F32)] * OWN, axis=1)
    last_ref[...] = jnp.where(
        iota(shape, 0) == iota(shape, 1) // F, jnp.broadcast_to(wide, shape), 0.0
    ).astype(BF16)
    copies[3].wait()
    shape = (CH_ALL, NV)
    j = (sources_ref[...] + OWN // 2) % CH_ALL
    z = jnp.zeros_like(j)
    for place, member in enumerate(Z_ORDER):
        z = jnp.where((j // 16) % 16 == member, place, z)
    row = (j // 256) * 256 + ((j // 8) % 2) * 128 + (j % 8) * 16 + z
    one_hot_ref[...] = jnp.where(iota(shape, 0) == jnp.broadcast_to(row, shape), 1.0, 0.0).astype(BF16)
    copies[0].wait()
    for layer in range(LAYERS):
        for tap in range(3):
            taps = [conv_ref[layer, a, tap] for a in range(3)]
            base = jnp.concatenate(taps + [jnp.zeros((F, 256 - 3 * F), BF16)], axis=1)
            for c in range(BLK):
                row = base if c == 0 else pltpu.roll(base, F * c, 1)
                for block in range(2):
                    band_ref[layer, block, F * c : F * (c + 1), 256 * tap : 256 * (tap + 1)] = row

    @pl.when(cut_ref[0] == 1)
    def _():
        for layer in range(LAYERS):
            for block in range(2):
                start = block * (EXT - 2 * (layer + 1) - BLK) + layer
                for c, k in ((5 - start, 7 - start), (6 - start, 6 - start)):
                    if 0 <= c < BLK:
                        for tap in range(3):
                            lanes = slice(256 * tap + F * k, 256 * tap + F * (k + 1))
                            band_ref[layer, block, F * c : F * (c + 1), lanes] = jnp.zeros((F, F), BF16)

    for copy in copies[4:]:
        copy.wait()


def lane_shift(x, step):
    edge = iota((x.shape[0], LANES), 1) == (0 if step == 1 else LANES - 1)
    moved = [
        jnp.where(edge, jnp.zeros_like(part), pltpu.roll(part, step % LANES, 1))
        for part in (x[:, i : i + LANES] for i in range(0, x.shape[1], LANES))
    ]
    return jnp.concatenate(moved, axis=1)


def denoise_kernel(
    own_ref, left_ref, order_ref, band_ref, first_ref, last_ref, table_ref,
    out_ref, h0_ref, h1_ref, h2_ref, h3_ref, earlier_ref, later_ref, line_ref,
):
    rows = [ref[w, :, :NT].astype(F32) for w in range(WIN) for ref in (own_ref, left_ref)]
    rows = jnp.concatenate(rows, axis=0).astype(BF16)
    rows = jnp.dot(rows, order_ref[...], preferred_element_type=F32)
    lines = [
        jnp.concatenate(
            [rows[16 * w : 16 * (w + 1), v * LANES : (v + 1) * LANES] for w in range(WIN)], axis=1
        )
        for v in range(PH)
    ]
    hidden = (h0_ref, h1_ref, h2_ref, h3_ref)
    chunk = [slice(v * CHUNK, (v + 1) * CHUNK) for v in range(PH)]
    for v in range(PH):
        before = lines[v - 1] if v > 0 else lane_shift(lines[PH - 1], 1)
        after = lines[v + 1] if v < PH - 1 else lane_shift(lines[0], -1)
        taps = jnp.concatenate([before, lines[v], after], axis=0).astype(BF16)
        h0_ref[:, chunk[v]] = jnp.dot(first_ref[...], taps, preferred_element_type=F32).astype(BF16)
    for layer in range(LAYERS):
        step = 2**layer
        source, target = hidden[layer], hidden[layer + 1]
        size = (EXT - 2 * layer) * F
        count = EXT - 2 * (layer + 1)
        for v in sorted(range(PH), key=lambda v: (v < step) + (v >= PH - step)):
            before, after, u, t = source, source, v - step, v + step
            if u < 0:
                u += PH
                before = earlier_ref
                earlier_ref[:size, chunk[u]] = lane_shift(source[:, chunk[u]], 1)
            if t >= PH:
                t -= PH
                after = later_ref
                later_ref[:size, chunk[t]] = lane_shift(source[:, chunk[t]], -1)
            for block, start, low in ((0, 0, 0), (1, count - BLK, 2 * BLK - count)):
                k = slice(start * F, (start + BLK + 2) * F)
                taps = jnp.concatenate([before[k, chunk[u]], source[k, chunk[v]], after[k, chunk[t]]], axis=0)
                total = jnp.dot(band_ref[layer, block, low * F :, :], taps, preferred_element_type=F32)
                old = source[(start + low + 1) * F : (start + BLK + 1) * F, chunk[v]].astype(F32)
                new = old + jnp.maximum(total, 0.0)
                for i in range(BLK - low):
                    c = start + low + i
                    target[c * F : (c + 1) * F, chunk[v]] = new[i * F : (i + 1) * F].astype(BF16)
    clean = jnp.dot(last_ref[...], h3_ref[...], preferred_element_type=F32)
    clean = jnp.concatenate(
        [
            jnp.concatenate(
                [clean[:, v * CHUNK + w * LANES : v * CHUNK + (w + 1) * LANES] for v in range(PH)], axis=1
            )
            for w in range(WIN)
        ],
        axis=0,
    )
    spectra = jnp.dot(clean.astype(BF16), table_ref[...], preferred_element_type=F32)
    real, imag = spectra[:, :NF], spectra[:, NF:]
    power = real * real + imag * imag
    spread = jnp.sqrt(jnp.mean(power, axis=1, keepdims=True) + epsilon_power)
    flags = jnp.concatenate(
        [
            ref[w, :, NT : NT + 1].astype(F32)[part]
            for w in range(WIN)
            for ref, part in ((left_ref, slice(4, 8)), (own_ref, slice(0, 4)))
        ],
        axis=0,
    )
    factor = flags / (jnp.sqrt(power) + water_level * spread)
    for part, value in enumerate((real * factor, imag * factor)):
        for w in range(WIN):
            for high in range(2):
                x = value[w * OWN : (w + 1) * OWN, high * 128 : (high + 1) * 128]
                for bit in range(3):
                    x = swap_bits(x, 2**bit, 16 * 2**bit)
                line_ref[pl.ds(32 * high + 2 * w + part, 8, stride=4), :] = x
    out_ref[...] = line_ref[...].astype(BF16)


def turn_kernel(in_ref, out_ref):
    x = in_ref[...].astype(F32)
    for bit in range(4):
        x = swap_bits(x, 4 * 2**bit, 2**bit)
    x = x.astype(BF16)
    out_ref[:64, :] = x
    out_ref[64:, :] = x


def coherence_kernel(half_ref, one_hot_ref, perm_ref, in_ref, out_any, all_ref, out_ref, sems):
    x = in_ref[...].astype(F32)

    def piece(w, c, y):
        start = ((w * 2 + c) * 4 + Y_ORDER.index(y)) * 8
        return x[start : start + 8]

    stacked = jnp.concatenate(
        [
            jnp.concatenate([piece(w, c, y) for y in range(4) for w in range(2)], axis=0)
            for c in range(2)
        ],
        axis=1,
    ).astype(BF16)
    ordered = jnp.dot(stacked, perm_ref[...], preferred_element_type=F32)
    every = jnp.concatenate([ordered[16 * y : 16 * (y + 1)] for y in range(4)], axis=1)
    all_ref[...] = pltpu.roll(every, CH_ALL - OWN // 2, 1)
    half = half_ref[0]
    receivers = all_ref[:, pl.ds(pl.multiple_of(half * 512, 512), 512)]
    gathered = jnp.concatenate([stacked[16 * y : 16 * (y + 1)] for y in range(4)], axis=1)
    chosen = jnp.dot(gathered, one_hot_ref[...], preferred_element_type=F32)
    even = iota(receivers.shape, 0) % 2 == 0
    turned = jnp.where(even, pltpu.roll(receivers, 15, 0), -pltpu.roll(receivers, 1, 0))
    chosen_t = chosen.T
    energy_src = jnp.sum(chosen_t * chosen_t, axis=1, keepdims=True)
    energy_rec = jnp.sum(receivers * receivers, axis=0, keepdims=True)
    scale = lax.rsqrt(jnp.maximum(energy_src * energy_rec, 1.0))
    left = chosen_t.astype(BF16)
    copies = []
    for part, right in enumerate((receivers, turned)):
        out_ref[part] = jnp.dot(left, right.astype(BF16), preferred_element_type=F32) * scale
        copies.append(pltpu.make_async_copy(out_ref.at[part], out_any.at[0, part], sems.at[part]))
        copies[-1].start()
    for copy in copies:
        copy.wait()


VMEM = pl.BlockSpec(memory_space=pltpu.VMEM)
SMEM = pl.BlockSpec(memory_space=pltpu.SMEM)
PARAMS = pltpu.CompilerParams(vmem_limit_bytes=32 * 1024 * 1024)


def pack(raw, flags):
    raw, flags = (pltpu.with_memory_space_constraint(a, pltpu.HBM) for a in (raw, flags))
    return pl.pallas_call(
        pack_kernel,
        out_shape=jax.ShapeDtypeStruct((WIN, OWN, NT + LANES), BF16),
        in_specs=[pl.BlockSpec(memory_space=pl.ANY)] * 2,
        out_specs=VMEM,
        scratch_shapes=[pltpu.VMEM(flags.shape, flags.dtype), pltpu.SemaphoreType.DMA((2,))],
        compiler_params=PARAMS,
        name="pack",
    )(raw, flags)


def prepare(cut, conv_weight, in_weight, out_weight, sources):
    arrays = (
        conv_weight.transpose(0, 3, 4, 1, 2), in_weight.T, out_weight.reshape(1, F), sources.reshape(1, NV),
        jnp.asarray(sample_perm()), jnp.asarray(dft_table()), jnp.asarray(channel_perm()),
    )
    arrays = tuple(pltpu.with_memory_space_constraint(a, pltpu.HBM) for a in arrays)
    return pl.pallas_call(
        prepare_kernel,
        out_shape=(
            jax.ShapeDtypeStruct((LAYERS, 2, BLK * F, 3 * 256), BF16),
            jax.ShapeDtypeStruct((EXT * F, 48), BF16),
            jax.ShapeDtypeStruct((OWN, OWN * F), BF16),
            jax.ShapeDtypeStruct((CH_ALL, NV), BF16),
        )
        + tuple(jax.ShapeDtypeStruct(a.shape, a.dtype) for a in arrays[4:]),
        in_specs=[SMEM] + [pl.BlockSpec(memory_space=pl.ANY)] * 7,
        out_specs=(VMEM,) * 7,
        scratch_shapes=[pltpu.VMEM(a.shape, a.dtype) for a in arrays[:4]]
        + [pltpu.SemaphoreType.DMA((7,))],
        compiler_params=PARAMS,
        cost_estimate=pl.CostEstimate(flops=2_000_000, bytes_accessed=4_000_000, transcendentals=0),
        name="prepare",
    )(cut, *arrays)


def denoise(own, left, order, band, first, last, table):
    return pl.pallas_call(
        denoise_kernel,
        out_shape=jax.ShapeDtypeStruct((64, 128), BF16),
        in_specs=[VMEM] * 7,
        out_specs=VMEM,
        scratch_shapes=[pltpu.VMEM(((EXT - 2 * i) * F, WIDE), BF16) for i in range(LAYERS + 1)]
        + [pltpu.VMEM((EXT * F, WIDE), BF16)] * 2
        + [pltpu.VMEM((64, 128), F32)],
        compiler_params=PARAMS,
        name="denoise",
    )(own, left, order, band, first, last, table)


def turn(rows):
    return pl.pallas_call(
        turn_kernel,
        out_shape=jax.ShapeDtypeStruct((128, 128), BF16),
        in_specs=[VMEM],
        out_specs=VMEM,
        compiler_params=PARAMS,
        name="turn",
    )(rows)


def coherence(half, one_hot, perm, rows):
    return pl.pallas_call(
        coherence_kernel,
        out_shape=jax.ShapeDtypeStruct((1, 2, 128, 512), F32),
        in_specs=[SMEM, VMEM, VMEM, VMEM],
        out_specs=pl.BlockSpec(memory_space=pl.ANY),
        scratch_shapes=[
            pltpu.VMEM((16, CH_ALL), F32),
            pltpu.VMEM((2, 128, 512), F32),
            pltpu.SemaphoreType.DMA((2,)),
        ],
        compiler_params=PARAMS,
        name="coherence",
    )(half, one_hot, perm, rows)


CHAN = ("y", "z", "c")


def per_device(raw, flags, in_weight, conv_weight, out_weight, sources):
    count = lax.axis_size(CHAN)
    own = pack(raw, flags)
    left = lax.ppermute(own, CHAN, [(i, (i + 1) % count) for i in range(count)])
    cut = (lax.axis_index(CHAN) == 0).astype(jnp.int32).reshape(1)
    half = lax.axis_index("w").reshape(1).astype(jnp.int32)
    band, first, last, one_hot, order, table, perm = prepare(cut, conv_weight, in_weight, out_weight, sources)
    sent = denoise(own, left, order, band, first, last, table)
    half, sent = lax.optimization_barrier((half, sent))
    got = lax.all_to_all(
        sent, "z", 0, 0, tiled=True, axis_index_groups=[[int(z) for z in Z_ORDER]]
    )
    rest = [((w * 2 + c) * 4 + y) * 2 + s for w in W_ORDER for c in range(2) for y in Y_ORDER for s in range(2)]
    mine = lax.all_to_all(turn(got), ("w", "c", "y", "s"), 0, 0, tiled=True, axis_index_groups=[rest])
    return coherence(half, one_hot, perm, mine)


def solution(mesh):
    fine = Mesh(mesh.devices.reshape(2, 4, 16, 2, 2), ("s", "y", "z", "c", "w"))
    placed = (P(("s", "w"), CHAN, None), P(("s", "w"), CHAN), P(), P(), P(), P())
    return jax.shard_map(
        per_device,
        mesh=fine,
        in_specs=placed,
        out_specs=P(("s",) + CHAN, None, None, "w"),
        check_vma=False,
    )
```

```python
import functools
import math

import jax
import jax.numpy as jnp
import numpy as np
from jax import lax
from jax.experimental import pallas as pl
from jax.experimental.pallas import tpu as pltpu
from jax.sharding import Mesh, PartitionSpec as P

NT = 640
F = 32
LAYERS = 3
NF = 256
OWN = 8
WIN = 2
EXT = OWN + 2 * LAYERS
BLK = 6
LANES = 128
PH = NT // LANES
CHUNK = WIN * LANES
WIDE = WIN * NT
CH_ALL = 1024
NV = 128
Y_ORDER = (2, 0, 1, 3)
W_ORDER = (1, 0)
Z_ORDER = (8, 0, 1, 15, 2, 14, 3, 13, 4, 12, 5, 11, 6, 10, 7, 9)

water_level = 0.2
epsilon_power = 1e-06

F32 = jnp.float32
BF16 = jnp.bfloat16


def dft_table():
    part, z, core, y, section = np.meshgrid(
        np.arange(2), np.array(Z_ORDER), np.arange(2), np.array(Y_ORDER), np.arange(2), indexing="ij"
    )
    k = (section * 128 + (y * 16 + z) * 2 + core).reshape(-1)
    part = part.reshape(-1)
    phases = np.arange(NT)[:, None] * (k + 1)[None, :] % NT
    angles = phases.astype(np.float32) * np.float32(2.0 * math.pi / NT)
    table = np.where(part[None, :] == 0, np.cos(angles), -np.sin(angles))
    return table[sample_order()].astype(BF16)


def sample_order():
    return (np.arange(LANES)[None, :] * PH + np.arange(PH)[:, None]).reshape(-1)


def sample_perm():
    return np.eye(NT, dtype=np.float32)[:, sample_order()].astype(BF16)


def channel_perm():
    core, channel, z = np.meshgrid(np.arange(2), np.arange(OWN), np.array(Z_ORDER), indexing="ij")
    target = ((z * 2 + core) * OWN + channel).reshape(-1)
    return np.eye(256, dtype=np.float32)[target].astype(BF16)


def iota(shape, dim):
    return lax.broadcasted_iota(jnp.int32, shape, dim)


def column(row, n):
    eye = iota((n, n), 0) == iota((n, n), 1)
    return jnp.sum(jnp.where(eye, jnp.broadcast_to(row, (n, n)), 0.0), axis=1, keepdims=True)


def swap_bits(x, row_step, lane_step):
    rows, lanes = x.shape
    row_bit = (iota(x.shape, 0) // row_step) % 2
    lane_bit = (iota(x.shape, 1) // lane_step) % 2
    down = pltpu.roll(pltpu.roll(x, rows - row_step, 0), lane_step, 1)
    up = pltpu.roll(pltpu.roll(x, row_step, 0), lanes - lane_step, 1)
    return jnp.where(row_bit == lane_bit, x, jnp.where(row_bit == 0, down, up))


def pack_kernel(raw_any, flags_any, own_ref, flags_ref, sems):
    copies = (
        pltpu.make_async_copy(flags_any, flags_ref, sems.at[0]),
        pltpu.make_async_copy(raw_any, own_ref.at[:, :, pl.ds(0, NT)], sems.at[1]),
    )
    for copy in copies:
        copy.start()
    copies[0].wait()
    for w in range(WIN):
        flags = column(flags_ref[w : w + 1, :].astype(F32), OWN)
        own_ref[w, :, NT:] = jnp.broadcast_to(flags, (OWN, LANES)).astype(BF16)
    copies[1].wait()


def prepare_kernel(
    cut_ref, conv_any, in_any, out_any, sources_any, order_any, table_any, perm_any,
    band_ref, first_ref, last_ref, one_hot_ref, order_ref, table_ref, perm_ref,
    conv_ref, in_ref, out_ref, sources_ref, sems,
):
    pairs = (
        (conv_any, conv_ref), (in_any, in_ref), (out_any, out_ref), (sources_any, sources_ref),
        (order_any, order_ref), (table_any, table_ref), (perm_any, perm_ref),
    )
    copies = [pltpu.make_async_copy(a, b, sems.at[i]) for i, (a, b) in enumerate(pairs)]
    for copy in copies:
        copy.start()
    copies[1].wait()
    shape = (EXT * F, 48)
    channel = iota(shape, 0) // F
    place = jnp.where(channel < 7, OWN + 1 + channel, channel - 7)
    lane = iota(shape, 1)
    first = jnp.zeros(shape, F32)
    for tap in range(3):
        weight = column(in_ref[tap : tap + 1, :].astype(F32), F)
        tall = jnp.broadcast_to(jnp.concatenate([weight] * EXT, axis=0), shape)
        first = jnp.where(lane == place + 16 * tap, tall, first)
    first_ref[...] = first.astype(BF16)
    copies[2].wait()
    shape = (OWN, OWN * F)
    wide = jnp.concatenate([out_ref[...].astype(F32)] * OWN, axis=1)
    last_ref[...] = jnp.where(
        iota(shape, 0) == iota(shape, 1) // F, jnp.broadcast_to(wide, shape), 0.0
    ).astype(BF16)
    copies[3].wait()
    shape = (CH_ALL, NV)
    j = (sources_ref[...] + OWN // 2) % CH_ALL
    z = jnp.zeros_like(j)
    for place, member in enumerate(Z_ORDER):
        z = jnp.where((j // 16) % 16 == member, place, z)
    row = (j // 256) * 256 + ((j // 8) % 2) * 128 + (j % 8) * 16 + z
    one_hot_ref[...] = jnp.where(iota(shape, 0) == jnp.broadcast_to(row, shape), 1.0, 0.0).astype(BF16)
    copies[0].wait()
    for layer in range(LAYERS):
        for tap in range(3):
            taps = [conv_ref[layer, a, tap] for a in range(3)]
            base = jnp.concatenate(taps + [jnp.zeros((F, 256 - 3 * F), BF16)], axis=1)
            for c in range(BLK):
                row = base if c == 0 else pltpu.roll(base, F * c, 1)
                for block in range(2):
                    band_ref[layer, block, F * c : F * (c + 1), 256 * tap : 256 * (tap + 1)] = row

    @pl.when(cut_ref[0] == 1)
    def _():
        for layer in range(LAYERS):
            for block in range(2):
                start = block * (EXT - 2 * (layer + 1) - BLK) + layer
                for c, k in ((5 - start, 7 - start), (6 - start, 6 - start)):
                    if 0 <= c < BLK:
                        for tap in range(3):
                            lanes = slice(256 * tap + F * k, 256 * tap + F * (k + 1))
                            band_ref[layer, block, F * c : F * (c + 1), lanes] = jnp.zeros((F, F), BF16)

    for copy in copies[4:]:
        copy.wait()


def lane_shift(x, step):
    edge = iota((x.shape[0], LANES), 1) == (0 if step == 1 else LANES - 1)
    moved = [
        jnp.where(edge, jnp.zeros_like(part), pltpu.roll(part, step % LANES, 1))
        for part in (x[:, i : i + LANES] for i in range(0, x.shape[1], LANES))
    ]
    return jnp.concatenate(moved, axis=1)


def denoise_kernel(
    own_ref, left_ref, order_ref, band_ref, first_ref, last_ref, table_ref,
    out_ref, h0_ref, h1_ref, h2_ref, h3_ref, earlier_ref, later_ref, line_ref,
):
    rows = [ref[w, :, :NT].astype(F32) for w in range(WIN) for ref in (own_ref, left_ref)]
    rows = jnp.concatenate(rows, axis=0).astype(BF16)
    rows = jnp.dot(rows, order_ref[...], preferred_element_type=F32)
    lines = [
        jnp.concatenate(
            [rows[16 * w : 16 * (w + 1), v * LANES : (v + 1) * LANES] for w in range(WIN)], axis=1
        )
        for v in range(PH)
    ]
    hidden = (h0_ref, h1_ref, h2_ref, h3_ref)
    chunk = [slice(v * CHUNK, (v + 1) * CHUNK) for v in range(PH)]
    for v in range(PH):
        before = lines[v - 1] if v > 0 else lane_shift(lines[PH - 1], 1)
        after = lines[v + 1] if v < PH - 1 else lane_shift(lines[0], -1)
        taps = jnp.concatenate([before, lines[v], after], axis=0).astype(BF16)
        h0_ref[:, chunk[v]] = jnp.dot(first_ref[...], taps, preferred_element_type=F32).astype(BF16)
    for layer in range(LAYERS):
        step = 2**layer
        source, target = hidden[layer], hidden[layer + 1]
        size = (EXT - 2 * layer) * F
        count = EXT - 2 * (layer + 1)
        for v in sorted(range(PH), key=lambda v: (v < step) + (v >= PH - step)):
            before, after, u, t = source, source, v - step, v + step
            if u < 0:
                u += PH
                before = earlier_ref
                earlier_ref[:size, chunk[u]] = lane_shift(source[:, chunk[u]], 1)
            if t >= PH:
                t -= PH
                after = later_ref
                later_ref[:size, chunk[t]] = lane_shift(source[:, chunk[t]], -1)
            for block, start, low in ((0, 0, 0), (1, count - BLK, 2 * BLK - count)):
                k = slice(start * F, (start + BLK + 2) * F)
                taps = jnp.concatenate([before[k, chunk[u]], source[k, chunk[v]], after[k, chunk[t]]], axis=0)
                total = jnp.dot(band_ref[layer, block, low * F :, :], taps, preferred_element_type=F32)
                old = source[(start + low + 1) * F : (start + BLK + 1) * F, chunk[v]].astype(F32)
                new = old + jnp.maximum(total, 0.0)
                for i in range(BLK - low):
                    c = start + low + i
                    target[c * F : (c + 1) * F, chunk[v]] = new[i * F : (i + 1) * F].astype(BF16)
    clean = jnp.dot(last_ref[...], h3_ref[...], preferred_element_type=F32)
    clean = jnp.concatenate(
        [
            jnp.concatenate(
                [clean[:, v * CHUNK + w * LANES : v * CHUNK + (w + 1) * LANES] for v in range(PH)], axis=1
            )
            for w in range(WIN)
        ],
        axis=0,
    )
    spectra = jnp.dot(clean.astype(BF16), table_ref[...], preferred_element_type=F32)
    real, imag = spectra[:, :NF], spectra[:, NF:]
    power = real * real + imag * imag
    spread = jnp.sqrt(jnp.mean(power, axis=1, keepdims=True) + epsilon_power)
    flags = jnp.concatenate(
        [
            ref[w, :, NT : NT + 1].astype(F32)[part]
            for w in range(WIN)
            for ref, part in ((left_ref, slice(4, 8)), (own_ref, slice(0, 4)))
        ],
        axis=0,
    )
    factor = flags / (jnp.sqrt(power) + water_level * spread)
    for part, value in enumerate((real * factor, imag * factor)):
        for w in range(WIN):
            for high in range(2):
                x = value[w * OWN : (w + 1) * OWN, high * 128 : (high + 1) * 128]
                for bit in range(3):
                    x = swap_bits(x, 2**bit, 16 * 2**bit)
                line_ref[pl.ds(32 * high + 2 * w + part, 8, stride=4), :] = x
    out_ref[...] = line_ref[...].astype(BF16)


def turn_kernel(in_ref, out_ref):
    x = in_ref[...].astype(F32)
    for bit in range(4):
        x = swap_bits(x, 4 * 2**bit, 2**bit)
    x = x.astype(BF16)
    out_ref[:64, :] = x
    out_ref[64:, :] = x


def coherence_kernel(half_ref, one_hot_ref, perm_ref, in_ref, out_any, all_ref, out_ref, sems):
    x = in_ref[...].astype(F32)

    def piece(w, c, y):
        start = ((w * 2 + c) * 4 + Y_ORDER.index(y)) * 8
        return x[start : start + 8]

    stacked = jnp.concatenate(
        [
            jnp.concatenate([piece(w, c, y) for y in range(4) for w in range(2)], axis=0)
            for c in range(2)
        ],
        axis=1,
    ).astype(BF16)
    ordered = jnp.dot(stacked, perm_ref[...], preferred_element_type=F32)
    every = jnp.concatenate([ordered[16 * y : 16 * (y + 1)] for y in range(4)], axis=1)
    all_ref[...] = pltpu.roll(every, CH_ALL - OWN // 2, 1)
    half = half_ref[0]
    receivers = all_ref[:, pl.ds(pl.multiple_of(half * 512, 512), 512)]
    gathered = jnp.concatenate([stacked[16 * y : 16 * (y + 1)] for y in range(4)], axis=1)
    chosen = jnp.dot(gathered, one_hot_ref[...], preferred_element_type=F32)
    even = iota(receivers.shape, 0) % 2 == 0
    turned = jnp.where(even, pltpu.roll(receivers, 15, 0), -pltpu.roll(receivers, 1, 0))
    chosen_t = chosen.T
    energy_src = jnp.sum(chosen_t * chosen_t, axis=1, keepdims=True)
    energy_rec = jnp.sum(receivers * receivers, axis=0, keepdims=True)
    scale = lax.rsqrt(jnp.maximum(energy_src * energy_rec, 1.0))
    left = chosen_t.astype(BF16)
    copies = []
    for part, right in enumerate((receivers, turned)):
        out_ref[part] = jnp.dot(left, right.astype(BF16), preferred_element_type=F32) * scale
        copies.append(pltpu.make_async_copy(out_ref.at[part], out_any.at[0, part], sems.at[part]))
        copies[-1].start()
    for copy in copies:
        copy.wait()


VMEM = pl.BlockSpec(memory_space=pltpu.VMEM)
SMEM = pl.BlockSpec(memory_space=pltpu.SMEM)
PARAMS = pltpu.CompilerParams(vmem_limit_bytes=32 * 1024 * 1024)


def pack(raw, flags):
    raw, flags = (pltpu.with_memory_space_constraint(a, pltpu.HBM) for a in (raw, flags))
    return pl.pallas_call(
        pack_kernel,
        out_shape=jax.ShapeDtypeStruct((WIN, OWN, NT + LANES), BF16),
        in_specs=[pl.BlockSpec(memory_space=pl.ANY)] * 2,
        out_specs=VMEM,
        scratch_shapes=[pltpu.VMEM(flags.shape, flags.dtype), pltpu.SemaphoreType.DMA((2,))],
        compiler_params=PARAMS,
        name="pack",
    )(raw, flags)


def prepare(cut, conv_weight, in_weight, out_weight, sources):
    arrays = (
        conv_weight.transpose(0, 3, 4, 1, 2), in_weight.T, out_weight.reshape(1, F), sources.reshape(1, NV),
        jnp.asarray(sample_perm()), jnp.asarray(dft_table()), jnp.asarray(channel_perm()),
    )
    arrays = tuple(pltpu.with_memory_space_constraint(a, pltpu.HBM) for a in arrays)
    return pl.pallas_call(
        prepare_kernel,
        out_shape=(
            jax.ShapeDtypeStruct((LAYERS, 2, BLK * F, 3 * 256), BF16),
            jax.ShapeDtypeStruct((EXT * F, 48), BF16),
            jax.ShapeDtypeStruct((OWN, OWN * F), BF16),
            jax.ShapeDtypeStruct((CH_ALL, NV), BF16),
        )
        + tuple(jax.ShapeDtypeStruct(a.shape, a.dtype) for a in arrays[4:]),
        in_specs=[SMEM] + [pl.BlockSpec(memory_space=pl.ANY)] * 7,
        out_specs=(VMEM,) * 7,
        scratch_shapes=[pltpu.VMEM(a.shape, a.dtype) for a in arrays[:4]]
        + [pltpu.SemaphoreType.DMA((7,))],
        compiler_params=PARAMS,
        cost_estimate=pl.CostEstimate(flops=2_000_000, bytes_accessed=4_000_000, transcendentals=0),
        name="prepare",
    )(cut, *arrays)


def denoise(own, left, order, band, first, last, table):
    return pl.pallas_call(
        denoise_kernel,
        out_shape=jax.ShapeDtypeStruct((64, 128), BF16),
        in_specs=[VMEM] * 7,
        out_specs=VMEM,
        scratch_shapes=[pltpu.VMEM(((EXT - 2 * i) * F, WIDE), BF16) for i in range(LAYERS + 1)]
        + [pltpu.VMEM((EXT * F, WIDE), BF16)] * 2
        + [pltpu.VMEM((64, 128), F32)],
        compiler_params=PARAMS,
        name="denoise",
    )(own, left, order, band, first, last, table)


def turn(rows):
    return pl.pallas_call(
        turn_kernel,
        out_shape=jax.ShapeDtypeStruct((128, 128), BF16),
        in_specs=[VMEM],
        out_specs=VMEM,
        compiler_params=PARAMS,
        name="turn",
    )(rows)


def coherence(half, one_hot, perm, rows):
    return pl.pallas_call(
        coherence_kernel,
        out_shape=jax.ShapeDtypeStruct((1, 2, 128, 512), F32),
        in_specs=[SMEM, VMEM, VMEM, VMEM],
        out_specs=pl.BlockSpec(memory_space=pl.ANY),
        scratch_shapes=[
            pltpu.VMEM((16, CH_ALL), F32),
            pltpu.VMEM((2, 128, 512), F32),
            pltpu.SemaphoreType.DMA((2,)),
        ],
        compiler_params=PARAMS,
        name="coherence",
    )(half, one_hot, perm, rows)


CHAN = ("y", "z", "c")


def per_device(raw, flags, in_weight, conv_weight, out_weight, sources):
    count = lax.axis_size(CHAN)
    own = pack(raw, flags)
    left = lax.ppermute(own, CHAN, [(i, (i + 1) % count) for i in range(count)])
    cut = (lax.axis_index(CHAN) == 0).astype(jnp.int32).reshape(1)
    half = lax.axis_index("w").reshape(1).astype(jnp.int32)
    band, first, last, one_hot, order, table, perm = prepare(cut, conv_weight, in_weight, out_weight, sources)
    sent = denoise(own, left, order, band, first, last, table)
    half, sent = lax.optimization_barrier((half, sent))
    got = lax.all_to_all(
        sent, "z", 0, 0, tiled=True, axis_index_groups=[[int(z) for z in Z_ORDER]]
    )
    rest = [((w * 2 + c) * 4 + y) * 2 + s for w in W_ORDER for c in range(2) for y in Y_ORDER for s in range(2)]
    mine = lax.all_to_all(turn(got), ("w", "c", "y", "s"), 0, 0, tiled=True, axis_index_groups=[rest])
    return coherence(half, one_hot, perm, mine)


def solution(mesh):
    fine = Mesh(mesh.devices.reshape(2, 4, 16, 2, 2), ("s", "y", "z", "c", "w"))
    placed = (P(("s", "w"), CHAN, None), P(("s", "w"), CHAN), P(), P(), P(), P())
    return jax.shard_map(
        per_device,
        mesh=fine,
        in_specs=placed,
        out_specs=P(("s",) + CHAN, None, None, "w"),
        check_vma=False,
    )
```

```python
import functools
import math

import jax
import jax.numpy as jnp
import numpy as np
from jax import lax
from jax.experimental import pallas as pl
from jax.experimental.pallas import tpu as pltpu
from jax.sharding import Mesh, PartitionSpec as P

NT = 640
F = 32
LAYERS = 3
NF = 256
OWN = 8
WIN = 2
EXT = OWN + 2 * LAYERS
BLK = 6
LANES = 128
PH = NT // LANES
CHUNK = WIN * LANES
WIDE = WIN * NT
CH_ALL = 1024
NV = 128
Y_ORDER = (2, 3, 0, 1)
W_ORDER = (1, 0)
Z_ORDER = (8, 0, 1, 15, 2, 14, 3, 13, 4, 12, 5, 11, 6, 10, 7, 9)

water_level = 0.2
epsilon_power = 1e-06

F32 = jnp.float32
BF16 = jnp.bfloat16


def dft_table():
    part, z, core, y, section = np.meshgrid(
        np.arange(2), np.array(Z_ORDER), np.arange(2), np.array(Y_ORDER), np.arange(2), indexing="ij"
    )
    k = (section * 128 + (y * 16 + z) * 2 + core).reshape(-1)
    part = part.reshape(-1)
    phases = np.arange(NT)[:, None] * (k + 1)[None, :] % NT
    angles = phases.astype(np.float32) * np.float32(2.0 * math.pi / NT)
    table = np.where(part[None, :] == 0, np.cos(angles), -np.sin(angles))
    return table[sample_order()].astype(BF16)


def sample_order():
    return (np.arange(LANES)[None, :] * PH + np.arange(PH)[:, None]).reshape(-1)


def sample_perm():
    return np.eye(NT, dtype=np.float32)[:, sample_order()].astype(BF16)


def channel_perm():
    core, channel, z = np.meshgrid(np.arange(2), np.arange(OWN), np.array(Z_ORDER), indexing="ij")
    target = ((z * 2 + core) * OWN + channel).reshape(-1)
    return np.eye(256, dtype=np.float32)[target].astype(BF16)


def iota(shape, dim):
    return lax.broadcasted_iota(jnp.int32, shape, dim)


def column(row, n):
    eye = iota((n, n), 0) == iota((n, n), 1)
    return jnp.sum(jnp.where(eye, jnp.broadcast_to(row, (n, n)), 0.0), axis=1, keepdims=True)


def swap_bits(x, row_step, lane_step):
    rows, lanes = x.shape
    row_bit = (iota(x.shape, 0) // row_step) % 2
    lane_bit = (iota(x.shape, 1) // lane_step) % 2
    down = pltpu.roll(pltpu.roll(x, rows - row_step, 0), lane_step, 1)
    up = pltpu.roll(pltpu.roll(x, row_step, 0), lanes - lane_step, 1)
    return jnp.where(row_bit == lane_bit, x, jnp.where(row_bit == 0, down, up))


def pack_kernel(raw_any, flags_any, own_ref, flags_ref, sems):
    copies = (
        pltpu.make_async_copy(flags_any, flags_ref, sems.at[0]),
        pltpu.make_async_copy(raw_any, own_ref.at[:, :, pl.ds(0, NT)], sems.at[1]),
    )
    for copy in copies:
        copy.start()
    copies[0].wait()
    for w in range(WIN):
        flags = column(flags_ref[w : w + 1, :].astype(F32), OWN)
        own_ref[w, :, NT:] = jnp.broadcast_to(flags, (OWN, LANES)).astype(BF16)
    copies[1].wait()


def prepare_kernel(
    cut_ref, conv_any, in_any, out_any, sources_any, order_any, table_any, perm_any,
    band_ref, first_ref, last_ref, one_hot_ref, order_ref, table_ref, perm_ref,
    conv_ref, in_ref, out_ref, sources_ref, sems,
):
    pairs = (
        (conv_any, conv_ref), (in_any, in_ref), (out_any, out_ref), (sources_any, sources_ref),
        (order_any, order_ref), (table_any, table_ref), (perm_any, perm_ref),
    )
    copies = [pltpu.make_async_copy(a, b, sems.at[i]) for i, (a, b) in enumerate(pairs)]
    for copy in copies:
        copy.start()
    copies[1].wait()
    shape = (EXT * F, 48)
    channel = iota(shape, 0) // F
    place = jnp.where(channel < 7, OWN + 1 + channel, channel - 7)
    lane = iota(shape, 1)
    first = jnp.zeros(shape, F32)
    for tap in range(3):
        weight = column(in_ref[tap : tap + 1, :].astype(F32), F)
        tall = jnp.broadcast_to(jnp.concatenate([weight] * EXT, axis=0), shape)
        first = jnp.where(lane == place + 16 * tap, tall, first)
    first_ref[...] = first.astype(BF16)
    copies[2].wait()
    shape = (OWN, OWN * F)
    wide = jnp.concatenate([out_ref[...].astype(F32)] * OWN, axis=1)
    last_ref[...] = jnp.where(
        iota(shape, 0) == iota(shape, 1) // F, jnp.broadcast_to(wide, shape), 0.0
    ).astype(BF16)
    copies[3].wait()
    shape = (CH_ALL, NV)
    j = (sources_ref[...] + OWN // 2) % CH_ALL
    z = jnp.zeros_like(j)
    for place, member in enumerate(Z_ORDER):
        z = jnp.where((j // 16) % 16 == member, place, z)
    row = (j // 256) * 256 + ((j // 8) % 2) * 128 + (j % 8) * 16 + z
    one_hot_ref[...] = jnp.where(iota(shape, 0) == jnp.broadcast_to(row, shape), 1.0, 0.0).astype(BF16)
    copies[0].wait()
    for layer in range(LAYERS):
        for tap in range(3):
            taps = [conv_ref[layer, a, tap] for a in range(3)]
            base = jnp.concatenate(taps + [jnp.zeros((F, 256 - 3 * F), BF16)], axis=1)
            for c in range(BLK):
                row = base if c == 0 else pltpu.roll(base, F * c, 1)
                for block in range(2):
                    band_ref[layer, block, F * c : F * (c + 1), 256 * tap : 256 * (tap + 1)] = row

    @pl.when(cut_ref[0] == 1)
    def _():
        for layer in range(LAYERS):
            for block in range(2):
                start = block * (EXT - 2 * (layer + 1) - BLK) + layer
                for c, k in ((5 - start, 7 - start), (6 - start, 6 - start)):
                    if 0 <= c < BLK:
                        for tap in range(3):
                            lanes = slice(256 * tap + F * k, 256 * tap + F * (k + 1))
                            band_ref[layer, block, F * c : F * (c + 1), lanes] = jnp.zeros((F, F), BF16)

    for copy in copies[4:]:
        copy.wait()


def lane_shift(x, step):
    edge = iota((x.shape[0], LANES), 1) == (0 if step == 1 else LANES - 1)
    moved = [
        jnp.where(edge, jnp.zeros_like(part), pltpu.roll(part, step % LANES, 1))
        for part in (x[:, i : i + LANES] for i in range(0, x.shape[1], LANES))
    ]
    return jnp.concatenate(moved, axis=1)


def denoise_kernel(
    own_ref, left_ref, order_ref, band_ref, first_ref, last_ref, table_ref,
    out_ref, h0_ref, h1_ref, h2_ref, h3_ref, earlier_ref, later_ref, line_ref,
):
    rows = [ref[w, :, :NT].astype(F32) for w in range(WIN) for ref in (own_ref, left_ref)]
    rows = jnp.concatenate(rows, axis=0).astype(BF16)
    rows = jnp.dot(rows, order_ref[...], preferred_element_type=F32)
    lines = [
        jnp.concatenate(
            [rows[16 * w : 16 * (w + 1), v * LANES : (v + 1) * LANES] for w in range(WIN)], axis=1
        )
        for v in range(PH)
    ]
    hidden = (h0_ref, h1_ref, h2_ref, h3_ref)
    chunk = [slice(v * CHUNK, (v + 1) * CHUNK) for v in range(PH)]
    for v in range(PH):
        before = lines[v - 1] if v > 0 else lane_shift(lines[PH - 1], 1)
        after = lines[v + 1] if v < PH - 1 else lane_shift(lines[0], -1)
        taps = jnp.concatenate([before, lines[v], after], axis=0).astype(BF16)
        h0_ref[:, chunk[v]] = jnp.dot(first_ref[...], taps, preferred_element_type=F32).astype(BF16)
    for layer in range(LAYERS):
        step = 2**layer
        source, target = hidden[layer], hidden[layer + 1]
        size = (EXT - 2 * layer) * F
        count = EXT - 2 * (layer + 1)
        for v in sorted(range(PH), key=lambda v: (v < step) + (v >= PH - step)):
            before, after, u, t = source, source, v - step, v + step
            if u < 0:
                u += PH
                before = earlier_ref
                earlier_ref[:size, chunk[u]] = lane_shift(source[:, chunk[u]], 1)
            if t >= PH:
                t -= PH
                after = later_ref
                later_ref[:size, chunk[t]] = lane_shift(source[:, chunk[t]], -1)
            for block, start, low in ((0, 0, 0), (1, count - BLK, 2 * BLK - count)):
                k = slice(start * F, (start + BLK + 2) * F)
                taps = jnp.concatenate([before[k, chunk[u]], source[k, chunk[v]], after[k, chunk[t]]], axis=0)
                total = jnp.dot(band_ref[layer, block, low * F :, :], taps, preferred_element_type=F32)
                old = source[(start + low + 1) * F : (start + BLK + 1) * F, chunk[v]].astype(F32)
                new = old + jnp.maximum(total, 0.0)
                for i in range(BLK - low):
                    c = start + low + i
                    target[c * F : (c + 1) * F, chunk[v]] = new[i * F : (i + 1) * F].astype(BF16)
    clean = jnp.dot(last_ref[...], h3_ref[...], preferred_element_type=F32)
    clean = jnp.concatenate(
        [
            jnp.concatenate(
                [clean[:, v * CHUNK + w * LANES : v * CHUNK + (w + 1) * LANES] for v in range(PH)], axis=1
            )
            for w in range(WIN)
        ],
        axis=0,
    )
    spectra = jnp.dot(clean.astype(BF16), table_ref[...], preferred_element_type=F32)
    real, imag = spectra[:, :NF], spectra[:, NF:]
    power = real * real + imag * imag
    spread = jnp.sqrt(jnp.mean(power, axis=1, keepdims=True) + epsilon_power)
    flags = jnp.concatenate(
        [
            ref[w, :, NT : NT + 1].astype(F32)[part]
            for w in range(WIN)
            for ref, part in ((left_ref, slice(4, 8)), (own_ref, slice(0, 4)))
        ],
        axis=0,
    )
    factor = flags / (jnp.sqrt(power) + water_level * spread)
    for part, value in enumerate((real * factor, imag * factor)):
        for w in range(WIN):
            for high in range(2):
                x = value[w * OWN : (w + 1) * OWN, high * 128 : (high + 1) * 128]
                for bit in range(3):
                    x = swap_bits(x, 2**bit, 16 * 2**bit)
                line_ref[pl.ds(32 * high + 2 * w + part, 8, stride=4), :] = x
    out_ref[...] = line_ref[...].astype(BF16)


def turn_kernel(in_ref, out_ref):
    x = in_ref[...].astype(F32)
    for bit in range(4):
        x = swap_bits(x, 4 * 2**bit, 2**bit)
    x = x.astype(BF16)
    out_ref[:64, :] = x
    out_ref[64:, :] = x


def coherence_kernel(half_ref, one_hot_ref, perm_ref, in_ref, out_any, all_ref, out_ref, sems):
    x = in_ref[...].astype(F32)

    def piece(w, c, y):
        start = ((w * 2 + c) * 4 + Y_ORDER.index(y)) * 8
        return x[start : start + 8]

    stacked = jnp.concatenate(
        [
            jnp.concatenate([piece(w, c, y) for y in range(4) for w in range(2)], axis=0)
            for c in range(2)
        ],
        axis=1,
    ).astype(BF16)
    ordered = jnp.dot(stacked, perm_ref[...], preferred_element_type=F32)
    every = jnp.concatenate([ordered[16 * y : 16 * (y + 1)] for y in range(4)], axis=1)
    all_ref[...] = pltpu.roll(every, CH_ALL - OWN // 2, 1)
    half = half_ref[0]
    receivers = all_ref[:, pl.ds(pl.multiple_of(half * 512, 512), 512)]
    gathered = jnp.concatenate([stacked[16 * y : 16 * (y + 1)] for y in range(4)], axis=1)
    chosen = jnp.dot(gathered, one_hot_ref[...], preferred_element_type=F32)
    even = iota(receivers.shape, 0) % 2 == 0
    turned = jnp.where(even, pltpu.roll(receivers, 15, 0), -pltpu.roll(receivers, 1, 0))
    chosen_t = chosen.T
    energy_src = jnp.sum(chosen_t * chosen_t, axis=1, keepdims=True)
    energy_rec = jnp.sum(receivers * receivers, axis=0, keepdims=True)
    scale = lax.rsqrt(jnp.maximum(energy_src * energy_rec, 1.0))
    left = chosen_t.astype(BF16)
    copies = []
    for part, right in enumerate((receivers, turned)):
        right = right.astype(BF16)
        for i in range(2):
            rows = slice(i * 64, (i + 1) * 64)
            out_ref[part, rows] = jnp.dot(left[rows], right, preferred_element_type=F32) * scale[rows]
            copies.append(
                pltpu.make_async_copy(
                    out_ref.at[part, rows], out_any.at[0, part, rows], sems.at[2 * part + i]
                )
            )
            copies[-1].start()
    for copy in copies:
        copy.wait()


VMEM = pl.BlockSpec(memory_space=pltpu.VMEM)
SMEM = pl.BlockSpec(memory_space=pltpu.SMEM)
PARAMS = pltpu.CompilerParams(vmem_limit_bytes=32 * 1024 * 1024)


def pack(raw, flags):
    raw, flags = (pltpu.with_memory_space_constraint(a, pltpu.HBM) for a in (raw, flags))
    return pl.pallas_call(
        pack_kernel,
        out_shape=jax.ShapeDtypeStruct((WIN, OWN, NT + LANES), BF16),
        in_specs=[pl.BlockSpec(memory_space=pl.ANY)] * 2,
        out_specs=VMEM,
        scratch_shapes=[pltpu.VMEM(flags.shape, flags.dtype), pltpu.SemaphoreType.DMA((2,))],
        compiler_params=PARAMS,
        name="pack",
    )(raw, flags)


def prepare(cut, conv_weight, in_weight, out_weight, sources):
    arrays = (
        conv_weight.transpose(0, 3, 4, 1, 2), in_weight.T, out_weight.reshape(1, F), sources.reshape(1, NV),
        jnp.asarray(sample_perm()), jnp.asarray(dft_table()), jnp.asarray(channel_perm()),
    )
    arrays = tuple(pltpu.with_memory_space_constraint(a, pltpu.HBM) for a in arrays)
    return pl.pallas_call(
        prepare_kernel,
        out_shape=(
            jax.ShapeDtypeStruct((LAYERS, 2, BLK * F, 3 * 256), BF16),
            jax.ShapeDtypeStruct((EXT * F, 48), BF16),
            jax.ShapeDtypeStruct((OWN, OWN * F), BF16),
            jax.ShapeDtypeStruct((CH_ALL, NV), BF16),
        )
        + tuple(jax.ShapeDtypeStruct(a.shape, a.dtype) for a in arrays[4:]),
        in_specs=[SMEM] + [pl.BlockSpec(memory_space=pl.ANY)] * 7,
        out_specs=(VMEM,) * 7,
        scratch_shapes=[pltpu.VMEM(a.shape, a.dtype) for a in arrays[:4]]
        + [pltpu.SemaphoreType.DMA((7,))],
        compiler_params=PARAMS,
        cost_estimate=pl.CostEstimate(flops=2_000_000, bytes_accessed=4_000_000, transcendentals=0),
        name="prepare",
    )(cut, *arrays)


def denoise(own, left, order, band, first, last, table):
    return pl.pallas_call(
        denoise_kernel,
        out_shape=jax.ShapeDtypeStruct((64, 128), BF16),
        in_specs=[VMEM] * 7,
        out_specs=VMEM,
        scratch_shapes=[pltpu.VMEM(((EXT - 2 * i) * F, WIDE), BF16) for i in range(LAYERS + 1)]
        + [pltpu.VMEM((EXT * F, WIDE), BF16)] * 2
        + [pltpu.VMEM((64, 128), F32)],
        compiler_params=PARAMS,
        name="denoise",
    )(own, left, order, band, first, last, table)


def turn(rows):
    return pl.pallas_call(
        turn_kernel,
        out_shape=jax.ShapeDtypeStruct((128, 128), BF16),
        in_specs=[VMEM],
        out_specs=VMEM,
        compiler_params=PARAMS,
        name="turn",
    )(rows)


def coherence(half, one_hot, perm, rows):
    return pl.pallas_call(
        coherence_kernel,
        out_shape=jax.ShapeDtypeStruct((1, 2, 128, 512), F32),
        in_specs=[SMEM, VMEM, VMEM, VMEM],
        out_specs=pl.BlockSpec(memory_space=pl.ANY),
        scratch_shapes=[
            pltpu.VMEM((16, CH_ALL), F32),
            pltpu.VMEM((2, 128, 512), F32),
            pltpu.SemaphoreType.DMA((4,)),
        ],
        compiler_params=PARAMS,
        name="coherence",
    )(half, one_hot, perm, rows)


CHAN = ("y", "z", "c")


def per_device(raw, flags, in_weight, conv_weight, out_weight, sources):
    count = lax.axis_size(CHAN)
    own = pack(raw, flags)
    left = lax.ppermute(own, CHAN, [(i, (i + 1) % count) for i in range(count)])
    cut = (lax.axis_index(CHAN) == 0).astype(jnp.int32).reshape(1)
    half = lax.axis_index("w").reshape(1).astype(jnp.int32)
    band, first, last, one_hot, order, table, perm = prepare(cut, conv_weight, in_weight, out_weight, sources)
    sent = denoise(own, left, order, band, first, last, table)
    half, sent = lax.optimization_barrier((half, sent))
    got = lax.all_to_all(
        sent, "z", 0, 0, tiled=True, axis_index_groups=[[int(z) for z in Z_ORDER]]
    )
    rest = [((w * 2 + c) * 4 + y) * 2 + s for w in W_ORDER for c in range(2) for y in Y_ORDER for s in range(2)]
    mine = lax.all_to_all(turn(got), ("w", "c", "y", "s"), 0, 0, tiled=True, axis_index_groups=[rest])
    return coherence(half, one_hot, perm, mine)


def solution(mesh):
    fine = Mesh(mesh.devices.reshape(2, 4, 16, 2, 2), ("s", "y", "z", "c", "w"))
    placed = (P(("s", "w"), CHAN, None), P(("s", "w"), CHAN), P(), P(), P(), P())
    return jax.shard_map(
        per_device,
        mesh=fine,
        in_specs=placed,
        out_specs=P(("s",) + CHAN, None, None, "w"),
        check_vma=False,
    )
```
